256 devices in a mesh: row: 8 (over x, y_lo), col: 32 (over y_hi, z, core).
Axes of the slice: x: 4, y: 4 (y_hi: 2, y_lo: 2; y = y_hi * 2 + y_lo), z: 8, core: 2. Of those that a mesh axis runs over, the one named last changes fastest.
Arguments:
- theta_hat: float32 [256, 2, 256, 512], P('row', None, 'col'), may hold values from -6 to 6
- velocity: float32 [3, 256, 512, 512], P(None, 'row', 'col'), may hold values from -6 to 6
- wall_derivative: float32 [512, 512], replicated, may hold values from -0.25 to 0.25
- to_basis: float32 [512, 512], replicated, may hold values from -0.25 to 0.25
- from_basis: float32 [512, 512], replicated, may hold values from -0.25 to 0.25
- eigenvalues: float32 [512], replicated, may hold values from 0.05 to 20
Outputs:
- theta_next: float32 [256, 2, 256, 512], P('row', None, 'col')
The draws below stay inside these ranges and needn't reach their ends.
All inputs are finite; a program needn't handle non-finite values.
Results may differ from the reference program's by a relative error of at most 0.00005.
Values sent between devices are 32-bit elements; how exact they have to be, the bound alone decides.
A program may use at most 128 MiB of HBM per device.

```python
import math
import jax
import jax.numpy as jnp
from jax import lax

NX = 512
NY = 512
NZ = 256
KX = 256


def levels(own_key, shape, cuts, low, top_value):
    def one(axis_at, parts):
        heights = jax.random.uniform(jax.random.fold_in(jax.random.fold_in(own_key, 6), axis_at), (parts,), jnp.float32, low / len(cuts), top_value / len(cuts))
        return jnp.repeat(jnp.exp(heights), shape[axis_at] // parts).reshape((-1,) + (1,) * (len(shape) - axis_at - 1))

    loudness = one(*cuts[0])
    for cut in cuts[1:]:
        loudness = loudness * one(*cut)
    return loudness


def bell_draw(key, dims, scale, limit, cuts=(), held_as=jnp.bfloat16):
    loudness = levels(key, dims, cuts, -0.22, 0.18) if cuts else 1.0
    values = jax.random.normal(key, dims, jnp.float32) * scale * loudness
    return jnp.minimum(jnp.maximum(values, -limit), limit).astype(held_as)


def setup_inputs(seed: int = 0) -> dict:
    key_of = jax.random.split(jax.random.key(seed), 7)
    theta_hat = bell_draw(key_of[0], (KX, 2, NZ, NY), 1.0, 6.0, ((0, 8), (2, 32)), jnp.float32)
    velocity = bell_draw(key_of[1], (3, NZ, NY, NX), 1.0, 6.0, ((1, 8), (2, 32)), jnp.float32)
    wall_derivative = bell_draw(key_of[2], (NY, NY), NY ** -0.5, 0.25, (), jnp.float32)
    to_basis = bell_draw(key_of[3], (NY, NY), NY ** -0.5, 0.25, (), jnp.float32)
    from_basis = bell_draw(key_of[4], (NY, NY), NY ** -0.5, 0.25, (), jnp.float32)
    eigenvalues = jnp.clip(jnp.exp(jax.random.uniform(key_of[5], (NY,), jnp.float32, math.log(0.05), math.log(20.0))), 0.05, 20.0)
    return dict(theta_hat=theta_hat, velocity=velocity, wall_derivative=wall_derivative, to_basis=to_basis, from_basis=from_basis, eigenvalues=eigenvalues)


WAVE_ALONG = 0.01
WAVE_SPAN = 0.02
TIME_STEP = 0.25
DIFFUSIVITY = 2.0

def phase_pair(number_modes, length):
    modes = jnp.arange(number_modes, dtype=jnp.int32)
    points = jnp.arange(length, dtype=jnp.int32)
    turns = modes[:, None] * points[None, :] % length
    angle = turns.astype(jnp.float32) * (2.0 * math.pi / length)
    return (jnp.cos(angle), jnp.sin(angle))

def along_tables(number_modes, length):
    cosine, sine_part = phase_pair(number_modes, length)
    factor = math.sqrt(2.0 / length)
    wavenumber = WAVE_ALONG * jnp.arange(number_modes, dtype=jnp.int32).astype(jnp.float32)
    inverse = jnp.stack([factor * cosine, -factor * sine_part])
    derive = jnp.stack([-factor * wavenumber[:, None] * sine_part, -factor * wavenumber[:, None] * cosine])
    return (inverse, derive)

def span_numbers(length):
    modes = jnp.arange(length, dtype=jnp.int32)
    signed = jnp.where(modes < length // 2, modes, modes - length)
    return WAVE_SPAN * signed.astype(jnp.float32)

def span_tables(length):
    cosine, sine_part = phase_pair(length, length)
    factor = 1.0 / math.sqrt(length)
    rate = factor * span_numbers(length)[:, None]
    inverse = jnp.stack([jnp.stack([factor * cosine, factor * sine_part], axis=1), jnp.stack([-factor * sine_part, factor * cosine], axis=1)])
    derive = jnp.stack([jnp.stack([-rate * sine_part, rate * cosine], axis=1), jnp.stack([-rate * cosine, -rate * sine_part], axis=1)])
    forward = jnp.stack([jnp.stack([factor * cosine, -factor * sine_part], axis=1), jnp.stack([factor * sine_part, factor * cosine], axis=1)])
    return (inverse, derive, forward)

def reference(theta_hat, velocity, wall_derivative, to_basis, from_basis, eigenvalues):
    precise = lax.Precision.HIGHEST
    span_inverse, span_derive, span_forward = span_tables(NZ)
    along_inverse, along_derive = along_tables(KX, NX)
    slope_hat = jnp.einsum('acbj,ij->acbi', theta_hat, wall_derivative, precision=precise)
    theta_lines = jnp.einsum('ackj,ckdz->dazj', theta_hat, span_inverse, precision=precise)
    span_lines = jnp.einsum('ackj,ckdz->dazj', theta_hat, span_derive, precision=precise)
    slope_lines = jnp.einsum('ackj,ckdz->dazj', slope_hat, span_inverse, precision=precise)
    grad_along = jnp.einsum('dazj,dax->zjx', theta_lines, along_derive, precision=precise)
    grad_span = jnp.einsum('dazj,dax->zjx', span_lines, along_inverse, precision=precise)
    grad_wall = jnp.einsum('dazj,dax->zjx', slope_lines, along_inverse, precision=precise)
    advect = velocity[0] * grad_along + velocity[1] * grad_wall + velocity[2] * grad_span
    advect_lines = jnp.einsum('zjx,dax->dazj', advect, along_inverse, precision=precise)
    advect_hat = jnp.einsum('cazj,czdk->adkj', advect_lines, span_forward, precision=precise)
    right_side = theta_hat - TIME_STEP * advect_hat
    coefficients = jnp.einsum('adkj,ij->adki', right_side, to_basis, precision=precise)
    along_waves = WAVE_ALONG * jnp.arange(KX, dtype=jnp.int32).astype(jnp.float32)
    span_waves = span_numbers(NZ)
    divisor = 1.0 + TIME_STEP * DIFFUSIVITY * (along_waves[:, None, None, None] ** 2 + span_waves[None, None, :, None] ** 2 + eigenvalues[None, None, None, :])
    return jnp.einsum('adkj,ij->adki', coefficients / divisor, from_basis, precision=precise)
```

```python
import math

import jax
import jax.numpy as jnp
import ml_dtypes
import numpy as np
from jax import lax
from jax.experimental import pallas as pl
from jax.experimental.pallas import tpu as pltpu
from jax.sharding import PartitionSpec as P

NX = 512
NY = 512
NZ = 256
KX = 256
WAVE_ALONG = 0.01
WAVE_SPAN = 0.02
TIME_STEP = 0.25
DIFFUSIVITY = 2.0

F32 = jnp.float32
BF16 = jnp.bfloat16
MESH = pl.DeviceIdType.MESH
VMEM_LIMIT = 60 * 1024 * 1024


def split_table(table):
    table = table.astype(np.float32)
    high = table.astype(ml_dtypes.bfloat16)
    low = (table - high.astype(np.float32)).astype(ml_dtypes.bfloat16)
    return np.stack([high, low])


def span_tables():
    z = np.arange(NZ).reshape(4, 1, 64, 1, 1, 1)
    d = np.arange(2).reshape(1, 2, 1, 1, 1, 1)
    c = np.arange(2).reshape(1, 1, 1, 2, 1, 1)
    q = np.arange(NZ).reshape(32, 8).T.reshape(1, 1, 1, 1, 8, 32)
    angle = 2.0 * math.pi * ((z * q) % NZ) / NZ
    signed = WAVE_SPAN * np.where(q < NZ // 2, q, q - NZ)
    factor = 1.0 / math.sqrt(NZ)
    inverse = factor * np.cos(angle + 0.5 * math.pi * (c - d))
    derive = factor * signed * np.cos(angle + 0.5 * math.pi * (c + 1 - d))
    q = np.arange(NZ).reshape(32, 1, 8, 1, 1, 1)
    d = np.arange(2).reshape(1, 2, 1, 1, 1, 1)
    z = np.arange(NZ).reshape(1, 1, 1, 4, 1, 64)
    c = np.arange(2).reshape(1, 1, 1, 1, 2, 1)
    angle = -2.0 * math.pi * ((z * q) % NZ) / NZ
    forward = -TIME_STEP * factor * np.cos(angle + 0.5 * math.pi * (c - d))
    return [split_table(t.reshape(512, 512)) for t in (inverse, derive, forward)]


def along_tables():
    p = np.arange(KX).reshape(4, 2, 1, 32, 1)
    d = np.arange(2).reshape(1, 1, 2, 1, 1)
    x = np.arange(NX).reshape(1, 1, 1, 1, NX)
    angle = 2.0 * math.pi * ((p * x) % NX) / NX
    factor = math.sqrt(2.0 / NX)
    inverse = (factor * np.cos(angle + 0.5 * math.pi * d)).reshape(512, 512)
    derive = (factor * WAVE_ALONG * p * np.cos(angle + 0.5 * math.pi * (d + 1))).reshape(512, 512)
    return [split_table(t) for t in (inverse, derive, inverse.T)]


def split(value):
    high = value.astype(BF16)
    return high, (value - high.astype(F32)).astype(BF16)


def dot3(a, b, dims=(((1,), (0,)), ((), ()))):
    def one(u, v):
        return lax.dot_general(u, v, dims, preferred_element_type=F32)

    return one(a[0], b[0]) + (one(a[0], b[1]) + one(a[1], b[0]))


def regroup(v):
    lane = lax.broadcasted_iota(jnp.int32, v[0].shape, 1)
    low = lane < 64
    odd = (lane // 32) % 2 == 1
    a0 = jnp.where(low, v[0], pltpu.roll(v[2], 64, 1))
    a2 = jnp.where(low, pltpu.roll(v[0], 64, 1), v[2])
    a1 = jnp.where(low, v[1], pltpu.roll(v[3], 64, 1))
    a3 = jnp.where(low, pltpu.roll(v[1], 64, 1), v[3])
    return (
        jnp.where(odd, pltpu.roll(a1, 32, 1), a0),
        jnp.where(odd, a1, pltpu.roll(a0, 96, 1)),
        jnp.where(odd, pltpu.roll(a3, 32, 1), a2),
        jnp.where(odd, a3, pltpu.roll(a2, 96, 1)),
    )


def wrap(value, n):
    return jnp.where(value >= n, value - n, value)


def kernel(
    theta, velocity, wall, to_basis, from_basis, eig,
    span_inv_h, span_der_h, span_fwd_h, along_inv_h, along_der_h, along_fwd_h,
    out,
    th_v, t0, mat_v, tb_v, fb_v, eig_v, vel_v,
    span_inv, span_der, span_fwd, along_inv, along_der, along_fwd,
    d_hl, t_hl, tb_hl, fb_hl, inv_div,
    fs, fr, x_hl, xs, xr, y_hl, adv_hl, xbs, xbr, l_hl, bs, br, c_hl, ov,
    load_sem, vel_send, vel_recv, f_send, f_recv, x_send, x_recv, xb_send, xb_recv, b_send, b_recv, out_sem,
):
    row = lax.axis_index("row")
    col = lax.axis_index("col")
    mx = row // 2
    ml = row % 2
    me = col * 2 + ml

    loads = [
        pltpu.make_async_copy(s, d, load_sem.at[i])
        for i, (s, d) in enumerate(
            [
                (wall, mat_v), (span_inv_h, span_inv), (span_der_h, span_der),
                (along_inv_h, along_inv), (along_der_h, along_der), (along_fwd_h, along_fwd),
                (span_fwd_h, span_fwd), (to_basis, tb_v), (from_basis, fb_v), (eig, eig_v),
            ]
        )
    ]
    first = [
        pltpu.make_async_copy(theta.at[:, pl.ds(b * 128, 128)], th_v.at[b], load_sem.at[10 + b]) for b in range(4)
    ]
    own_vel = [
        pltpu.make_async_copy(
            velocity.at[:, :, pl.ds(pl.multiple_of(ml * 8, 8), 8), pl.ds(b * 128, 128)],
            vel_v.at[:, b, pl.ds(ml * 32, 32)],
            load_sem.at[14 + b],
        )
        for b in range(4)
    ]
    for copy in first + loads + own_vel:
        copy.start()

    barrier = pltpu.get_barrier_semaphore()

    def partner(k):
        other = wrap(me + k, 64)
        return other, {"row": mx * 2 + other % 2, "col": other // 2}

    def greet(k, carry):
        pl.semaphore_signal(barrier, inc=1, device_id=partner(k)[1], device_id_type=MESH)
        return carry

    lax.fori_loop(1, 64, greet, 0)
    for k in range(1, 4):
        pl.semaphore_signal(
            barrier, inc=1, device_id={"row": wrap(mx + k, 4) * 2 + ml, "col": col}, device_id_type=MESH
        )

    for b in range(4):
        first[b].wait()
        for g in range(4):
            block = jnp.concatenate([th_v[b, pl.ds(4 * g + i, 32, stride=16), :] for i in range(4)], axis=0)
            t0[g, pl.ds(b * 128, 128), :] = block.T

    sub = lax.broadcasted_iota(jnp.int32, (16, 8, 128), 1) < 4

    def blocks(f, i, value):
        value = [v.reshape(16, 8, 128) for v in value]
        rows = pl.ds(pl.multiple_of(i * 16, 16), 16)
        for g in range(2):
            left, right = value[g], value[2 + g]
            fs[f, 0, rows, pl.ds(g * 8, 8), :] = jnp.where(sub, left, pltpu.roll(right, 4, 1))
            fs[f, 1, rows, pl.ds(g * 8, 8), :] = jnp.where(sub, pltpu.roll(left, 4, 1), right)

    def theta_blocks(i, carry):
        rows = pl.ds(pl.multiple_of(i * 128, 128), 128)
        value = [t0[g, rows, :] for g in range(4)]
        blocks(0, i, value)
        for g in range(4):
            lanes = pl.ds(g * 128, 128)
            t_hl[0, rows, lanes], t_hl[1, rows, lanes] = split(value[g])
        return carry

    lax.fori_loop(0, 4, theta_blocks, 0)

    pl.semaphore_wait(barrier, 66)

    def send_fwd(f, c, velocity_too):
        mine = pl.ds(pl.multiple_of(me * 16, 16), 16)
        pltpu.make_async_copy(fs.at[f, c, me], fr.at[f, c, mine], f_recv.at[f, c]).start()

        def one(k, carry):
            other, device = partner(k)
            pltpu.make_async_remote_copy(
                src_ref=fs.at[f, c, other],
                dst_ref=fr.at[f, c, mine],
                send_sem=f_send.at[f, c],
                recv_sem=f_recv.at[f, c],
                device_id=device,
                device_id_type=MESH,
            ).start()
            return carry

        def piece(i, carry):
            lax.fori_loop(1 + 4 * i, jnp.minimum(5 + 4 * i, 64), one, 0)
            send_vel(i)
            return carry

        if velocity_too:
            lax.fori_loop(0, 16, piece, 0)
        else:
            lax.fori_loop(1, 64, one, 0)

    def send_vel(i):
        pltpu.make_async_remote_copy(
            src_ref=velocity.at[
                :,
                pl.ds(i % 4 * 8, 8),
                pl.ds(pl.multiple_of((1 - ml) * 8, 8), 8),
                pl.ds(pl.multiple_of(i // 4 * 128, 128), 128),
            ],
            dst_ref=vel_v.at[:, i // 4, pl.ds(ml * 32 + i % 4 * 8, 8)],
            send_sem=vel_send,
            recv_sem=vel_recv,
            device_id={"row": mx * 2 + 1 - ml, "col": col},
            device_id_type=MESH,
        ).start()

    send_fwd(0, 0, False)

    loads[0].wait()

    def slope(i, carry):
        r = pl.multiple_of(i * 128, 128)
        value = dot3(split(mat_v[pl.ds(r, 128), :]), (t_hl[0], t_hl[1]))
        blocks(1, i, [value[:, g * 128 : g * 128 + 128] for g in range(4)])
        return carry

    lax.fori_loop(0, 4, slope, 0)
    send_fwd(1, 0, False)
    send_fwd(0, 1, True)
    send_fwd(1, 1, False)

    for copy in loads[1:]:
        copy.wait()

    def halves(i, carry):
        r = pl.multiple_of(i * 64, 64)
        tb_hl[0, pl.ds(r, 64), :], tb_hl[1, pl.ds(r, 64), :] = split(tb_v[pl.ds(r, 64), :])
        fb_hl[0, pl.ds(r, 64), :], fb_hl[1, pl.ds(r, 64), :] = split(fb_v[pl.ds(r, 64), :])
        return carry

    lax.fori_loop(0, 8, halves, 0)
    lane = lax.broadcasted_iota(jnp.int32, (1, 512), 1)
    along_wave = WAVE_ALONG * (row * 32 + lane % 32).astype(F32)
    span_id = col * 8 + (lane // 32) % 8
    span_wave = WAVE_SPAN * jnp.where(span_id < NZ // 2, span_id, span_id - NZ).astype(F32)
    waves = along_wave * along_wave + span_wave * span_wave
    for kb in range(4):
        column = jnp.broadcast_to(eig_v[:, pl.ds(kb * 128, 128)], (128, 128)).T
        for g in range(4):
            total = waves[:, g * 128 : g * 128 + 128] + column
            inv_div[pl.ds(kb * 128, 128), pl.ds(g * 128, 128)] = 1.0 / (1.0 + TIME_STEP * DIFFUSIVITY * total)
    for copy in own_vel:
        copy.wait()

    def wait_all(ref, sem):
        pltpu.make_async_copy(ref, ref, sem).wait()

    def span_stage(f, c):
        wait_all(fr.at[f, c], f_recv.at[f, c])
        for yl in range(2):
            for qh in range(2):
                for g in range(2):
                    v = [
                        fr[f, c, pl.ds(yl * 16 + g * 8 + qh * 4 + j, 32, stride=32), :] for j in range(4)
                    ]
                    for i, u in enumerate(regroup(v)):
                        r = (qh * 8 + g * 4 + i) * 32
                        x_hl[0, pl.ds(r, 32), pl.ds(yl * 128, 128)], x_hl[1, pl.ds(r, 32), pl.ds(yl * 128, 128)] = split(u)

        def lift(table, h):
            def one(k, carry):
                other = wrap(mx + k, 4)
                r = pl.multiple_of(other * 128, 128)
                xs[c, h, pl.ds(r, 128), :] = dot3(
                    (table[0, pl.ds(r, 128), :], table[1, pl.ds(r, 128), :]), (x_hl[0], x_hl[1])
                )
                pltpu.make_async_remote_copy(
                    src_ref=xs.at[c, h, pl.ds(r, 128)],
                    dst_ref=xr.at[c, h, pl.ds(pl.multiple_of(mx * 128, 128), 128)],
                    send_sem=x_send.at[c, h],
                    recv_sem=x_recv.at[c, h],
                    device_id={"row": other * 2 + ml, "col": col},
                    device_id_type=MESH,
                ).start()
                return carry

            lax.fori_loop(1, 4, one, 0)
            r = pl.multiple_of(mx * 128, 128)
            xs[c, h, pl.ds(r, 128), :] = dot3(
                (table[0, pl.ds(r, 128), :], table[1, pl.ds(r, 128), :]), (x_hl[0], x_hl[1])
            )
            pltpu.make_async_copy(xs.at[c, h, pl.ds(r, 128)], xr.at[c, h, pl.ds(r, 128)], x_recv.at[c, h]).start()

        if f == 0:
            lift(span_inv, 0)
            lift(span_der, 1)
        else:
            lift(span_inv, 2)

    def gather_lines(c, h):
        wait_all(xr.at[c, h], x_recv.at[c, h])

        def one(x, carry):
            r = pl.multiple_of(x * 128, 128)
            v = [xr[c, h, pl.ds(r + d * 64, 64), pl.ds(yl * 128, 128)] for yl in range(2) for d in range(2)]
            for j, u in enumerate(regroup(v)):
                lanes = pl.ds(r, 128)
                y_hl[h, 0, pl.ds(j * 64, 64), lanes], y_hl[h, 1, pl.ds(j * 64, 64), lanes] = split(u)
            return carry

        lax.fori_loop(0, 4, one, 0)

    def along_stage(c):
        flat = vel_v.reshape(3, 4, 512, 128)
        for h in range(3):
            gather_lines(c, h)

        def one(n, carry):
            lanes = pl.ds(pl.multiple_of(n * 256, 256), 256)
            total = None
            for h, (table, component) in enumerate(((along_der, 0), (along_inv, 2), (along_inv, 1))):
                grad = dot3((y_hl[h, 0], y_hl[h, 1]), (table[0, :, lanes], table[1, :, lanes]))
                speed = jnp.concatenate(
                    [
                        jnp.concatenate(
                            [flat[component, 2 * n + b, pl.ds(4 * c + j, 64, stride=8), :] for j in range(4)], axis=0
                        )
                        for b in range(2)
                    ],
                    axis=1,
                )
                term = grad * speed
                total = term if total is None else total + term
            adv_hl[0, :, lanes], adv_hl[1, :, lanes] = split(total)
            return carry

        lax.fori_loop(0, 2, one, 0)

        def back(k, carry):
            other = wrap(mx + k, 4)
            r = pl.multiple_of(other * 128, 128)
            lanes = pl.ds(r, 128)
            modes = dot3((adv_hl[0], adv_hl[1]), (along_fwd[0, :, lanes], along_fwd[1, :, lanes]))
            v = regroup([modes[j * 64 : j * 64 + 64] for j in range(4)])
            for yl in range(2):
                for d in range(2):
                    xbs[c, pl.ds(r + d * 64, 64), pl.ds(yl * 128, 128)] = v[yl * 2 + d]

            @pl.when(k < 4)
            def _():
                pltpu.make_async_remote_copy(
                    src_ref=xbs.at[c, pl.ds(r, 128)],
                    dst_ref=xbr.at[c, pl.ds(pl.multiple_of(mx * 128, 128), 128)],
                    send_sem=xb_send.at[c],
                    recv_sem=xb_recv.at[c],
                    device_id={"row": other * 2 + ml, "col": col},
                    device_id_type=MESH,
                ).start()

            return carry

        lax.fori_loop(1, 5, back, 0)
        mine = pl.ds(pl.multiple_of(mx * 128, 128), 128)
        pltpu.make_async_copy(xbs.at[c, mine], xbr.at[c, mine], xb_recv.at[c]).start()

    def span_back_stage(c):
        wait_all(xbr.at[c], xb_recv.at[c])

        def halve(i, carry):
            rows = pl.ds(pl.multiple_of(i * 128, 128), 128)
            l_hl[0, rows, :], l_hl[1, rows, :] = split(xbr[c, rows, :])
            return carry

        lax.fori_loop(0, 4, halve, 0)

        def one(i, carry):
            rows = pl.ds(pl.multiple_of(i * 128, 128), 128)
            value = dot3((span_fwd[0, rows, :], span_fwd[1, rows, :]), (l_hl[0], l_hl[1]))
            bs[c, 0, rows, :] = value[:, :128]
            bs[c, 1, rows, :] = value[:, 128:]
            return carry

        lax.fori_loop(0, 4, one, 0)
        mine = pl.ds(pl.multiple_of(me * 16, 16), 16)
        pltpu.make_async_copy(
            bs.at[c, ml, pl.ds(pl.multiple_of(col * 16, 16), 16)], br.at[c, mine], b_recv.at[c]
        ).start()

        def send(k, carry):
            other, device = partner(k)
            pltpu.make_async_remote_copy(
                src_ref=bs.at[c, other % 2, pl.ds(pl.multiple_of(other // 2 * 16, 16), 16)],
                dst_ref=br.at[c, mine],
                send_sem=b_send.at[c],
                recv_sem=b_recv.at[c],
                device_id=device,
                device_id_type=MESH,
            ).start()
            return carry

        lax.fori_loop(1, 64, send, 0)

    def collect(c):
        wait_all(br.at[c], b_recv.at[c])
        for g in range(4):
            v = [br[c, pl.ds(4 * g + i, 64, stride=16), :] for i in range(4)]
            for j, u in enumerate(regroup(v)):
                rows = pl.ds(4 * c + j, 64, stride=8)
                t0[g, rows, :] = t0[g, rows, :] + u

    span_stage(0, 0)
    span_stage(1, 0)
    wait_all(vel_v.at[:, :, pl.ds(0, 32)], vel_recv)
    along_stage(0)
    span_back_stage(0)
    span_stage(0, 1)
    span_stage(1, 1)
    collect(0)
    along_stage(1)
    span_back_stage(1)
    collect(1)

    def halve_right(i, carry):
        rows = pl.ds(pl.multiple_of(i * 64, 64), 64)
        for g in range(4):
            lanes = pl.ds(g * 128, 128)
            t_hl[0, rows, lanes], t_hl[1, rows, lanes] = split(t0[g, rows, :])
        return carry

    lax.fori_loop(0, 8, halve_right, 0)

    def basis(i, carry):
        rows = pl.ds(pl.multiple_of(i * 128, 128), 128)
        value = dot3((tb_hl[0, rows, :], tb_hl[1, rows, :]), (t_hl[0], t_hl[1])) * inv_div[rows, :]
        for g in range(4):
            turned = value[:, g * 128 : g * 128 + 128].T
            c_hl[0, pl.ds(g * 128, 128), rows], c_hl[1, pl.ds(g * 128, 128), rows] = split(turned)
        return carry

    lax.fori_loop(0, 4, basis, 0)

    def last(g, carry):
        rows = pl.ds(pl.multiple_of(g * 128, 128), 128)
        value = dot3(
            (c_hl[0, rows, :], c_hl[1, rows, :]), (fb_hl[0], fb_hl[1]), (((1,), (1,)), ((), ()))
        )
        for i in range(4):
            for b in range(4):
                ov[b, pl.ds(4 * g + i, 32, stride=16), :] = value[i * 32 : i * 32 + 32, b * 128 : b * 128 + 128]
        return carry

    lax.fori_loop(0, 4, last, 0)
    results = [pltpu.make_async_copy(ov.at[b], out.at[:, pl.ds(b * 128, 128)], out_sem.at[b]) for b in range(4)]
    for result in results:
        result.start()

    wait_all(vel_v.at[:, :, pl.ds(0, 32)], vel_send)
    for c in range(2):
        for f in range(2):
            wait_all(fs.at[f, c, pl.ds(0, 63)], f_send.at[f, c])
        for h in range(3):
            wait_all(xs.at[c, h, pl.ds(0, 384)], x_send.at[c, h])
        wait_all(xbs.at[c, pl.ds(0, 384)], xb_send.at[c])
        wait_all(br.at[c, pl.ds(0, 1008)], b_send.at[c])
    for result in results:
        result.wait()


def shards(theta_hat, velocity, wall_derivative, to_basis, from_basis, eigenvalues):
    tables = span_tables() + along_tables()
    tables = [jnp.asarray(t) for t in tables]
    vm = pltpu.VMEM
    table = vm((2, 512, 512), BF16)
    square = vm((512, 512), F32)
    blocked = vm((4, 512, 128), F32)
    dma = pltpu.SemaphoreType.DMA
    result = pl.pallas_call(
        kernel,
        out_shape=jax.ShapeDtypeStruct((512, 512), F32),
        in_specs=[pl.BlockSpec(memory_space=pl.ANY)] * 12,
        out_specs=pl.BlockSpec(memory_space=pl.ANY),
        scratch_shapes=[
            blocked, blocked, square, square, square, vm((1, 512), F32), vm((3, 4, 64, 8, 128), F32),
            table, table, table, table, table, table,
            table, table, table, table, square,
            vm((2, 2, 64, 16, 128), F32),
            vm((2, 2, 1024, 128), F32),
            vm((2, 512, 256), BF16),
            vm((2, 3, 512, 256), F32),
            vm((2, 3, 512, 256), F32),
            vm((3, 2, 256, 512), BF16),
            vm((2, 256, 512), BF16),
            vm((2, 512, 256), F32),
            vm((2, 512, 256), F32),
            vm((2, 512, 256), BF16),
            vm((2, 2, 512, 128), F32),
            vm((2, 1024, 128), F32),
            table,
            blocked,
            dma((18,)), dma(()), dma(()), dma((2, 2)), dma((2, 2)), dma((2, 3)), dma((2, 3)),
            dma((2,)), dma((2,)), dma((2,)), dma((2,)), dma((4,)),
        ],
        compiler_params=pltpu.CompilerParams(
            collective_id=0, has_side_effects=True, vmem_limit_bytes=VMEM_LIMIT
        ),
        cost_estimate=pl.CostEstimate(flops=8 * 10**9, bytes_accessed=16 * 2**20, transcendentals=0),
    )(
        theta_hat.reshape(512, 512), velocity, wall_derivative, to_basis, from_basis,
        eigenvalues.reshape(1, 512), *tables,
    )
    return result.reshape(32, 2, 8, 512)


def solution(mesh):
    return jax.shard_map(
        shards,
        mesh=mesh,
        in_specs=(P("row", None, "col", None), P(None, "row", "col", None), P(), P(), P(), P()),
        out_specs=P("row", None, "col", None),
        check_vma=False,
    )
```

```python
import math

import jax
import jax.numpy as jnp
import ml_dtypes
import numpy as np
from jax import lax
from jax.experimental import pallas as pl
from jax.experimental.pallas import tpu as pltpu
from jax.sharding import PartitionSpec as P

NX = 512
NY = 512
NZ = 256
KX = 256
WAVE_ALONG = 0.01
WAVE_SPAN = 0.02
TIME_STEP = 0.25
DIFFUSIVITY = 2.0

F32 = jnp.float32
BF16 = jnp.bfloat16
MESH = pl.DeviceIdType.MESH
VMEM_LIMIT = 60 * 1024 * 1024


def split_table(table):
    table = table.astype(np.float32)
    high = table.astype(ml_dtypes.bfloat16)
    low = (table - high.astype(np.float32)).astype(ml_dtypes.bfloat16)
    return np.stack([high, low])


def span_tables():
    z = np.arange(NZ).reshape(4, 1, 64, 1, 1, 1)
    d = np.arange(2).reshape(1, 2, 1, 1, 1, 1)
    c = np.arange(2).reshape(1, 1, 1, 2, 1, 1)
    q = np.arange(NZ).reshape(32, 8).T.reshape(1, 1, 1, 1, 8, 32)
    angle = 2.0 * math.pi * ((z * q) % NZ) / NZ
    signed = WAVE_SPAN * np.where(q < NZ // 2, q, q - NZ)
    factor = 1.0 / math.sqrt(NZ)
    inverse = factor * np.cos(angle + 0.5 * math.pi * (c - d))
    derive = factor * signed * np.cos(angle + 0.5 * math.pi * (c + 1 - d))
    q = np.arange(NZ).reshape(1, 32, 8, 1, 1, 1)
    d = np.arange(2).reshape(2, 1, 1, 1, 1, 1)
    z = np.arange(NZ).reshape(1, 1, 1, 4, 1, 64)
    c = np.arange(2).reshape(1, 1, 1, 1, 2, 1)
    angle = -2.0 * math.pi * ((z * q) % NZ) / NZ
    forward = -TIME_STEP * factor * np.cos(angle + 0.5 * math.pi * (c - d))
    return [split_table(t.reshape(512, 512)) for t in (inverse, derive, forward)]


def along_tables():
    p = np.arange(KX).reshape(2, 2, 2, 1, 32, 1).transpose(0, 2, 1, 3, 4, 5)
    d = np.arange(2).reshape(1, 1, 1, 2, 1, 1)
    x = np.arange(NX).reshape(1, 1, 1, 1, 1, NX)
    angle = 2.0 * math.pi * ((p * x) % NX) / NX
    factor = math.sqrt(2.0 / NX)
    inverse = (factor * np.cos(angle + 0.5 * math.pi * d)).reshape(512, 512)
    derive = (factor * WAVE_ALONG * p * np.cos(angle + 0.5 * math.pi * (d + 1))).reshape(512, 512)
    return [split_table(t) for t in (inverse, derive, inverse.T)]


def split(value):
    high = value.astype(BF16)
    return high, (value - high.astype(F32)).astype(BF16)


def dot3(a, b, dims=(((1,), (0,)), ((), ()))):
    def one(u, v):
        return lax.dot_general(u, v, dims, preferred_element_type=F32)

    return one(a[0], b[0]) + (one(a[0], b[1]) + one(a[1], b[0]))


def regroup(v):
    lane = lax.broadcasted_iota(jnp.int32, v[0].shape, 1)
    low = lane < 64
    odd = (lane // 32) % 2 == 1
    a0 = jnp.where(low, v[0], pltpu.roll(v[2], 64, 1))
    a2 = jnp.where(low, pltpu.roll(v[0], 64, 1), v[2])
    a1 = jnp.where(low, v[1], pltpu.roll(v[3], 64, 1))
    a3 = jnp.where(low, pltpu.roll(v[1], 64, 1), v[3])
    return (
        jnp.where(odd, pltpu.roll(a1, 32, 1), a0),
        jnp.where(odd, a1, pltpu.roll(a0, 96, 1)),
        jnp.where(odd, pltpu.roll(a3, 32, 1), a2),
        jnp.where(odd, a3, pltpu.roll(a2, 96, 1)),
    )


def wrap(value, n):
    return jnp.where(value >= n, value - n, value)


def kernel(
    theta, velocity, wall, to_basis, from_basis, eig,
    span_inv_h, span_der_h, span_fwd_h, along_inv_h, along_der_h, along_fwd_h,
    out,
    th_v, t0, mat_v, tb_v, fb_v, eig_v, vel_v,
    span_inv, span_der, span_fwd, along_inv, along_der, along_fwd,
    d_hl, t_hl, tb_hl, fb_hl, inv_div,
    fs, fr, x_hl, xs, xr, y_hl, adv_hl, xbs, xbr, bs, br, c_hl, ov,
    load_sem, vel_send, vel_recv, f_send, f_recv, x_send, x_recv, xb_send, xb_recv, b_send, b_recv, out_sem,
):
    row = lax.axis_index("row")
    col = lax.axis_index("col")
    mx = row // 2
    ml = row % 2
    me = col * 2 + ml

    loads = [
        pltpu.make_async_copy(s, d, load_sem.at[i])
        for i, (s, d) in enumerate(
            [
                (wall, mat_v), (span_inv_h, span_inv), (span_der_h, span_der),
                (along_inv_h, along_inv), (along_der_h, along_der), (along_fwd_h, along_fwd),
                (span_fwd_h, span_fwd), (to_basis, tb_v), (from_basis, fb_v), (eig, eig_v),
            ]
        )
    ]
    first = [
        pltpu.make_async_copy(theta.at[:, pl.ds(b * 128, 128)], th_v.at[b], load_sem.at[10 + b]) for b in range(4)
    ]
    own_vel = [
        pltpu.make_async_copy(
            velocity.at[:, :, pl.ds(pl.multiple_of(ml * 8, 8), 8), pl.ds(b * 128, 128)],
            vel_v.at[:, b, pl.ds(ml * 32, 32)],
            load_sem.at[14 + b],
        )
        for b in range(4)
    ]
    for copy in first + loads + own_vel:
        copy.start()

    barrier = pltpu.get_barrier_semaphore()

    def partner(k):
        other = wrap(me + k, 64)
        return other, {"row": mx * 2 + other % 2, "col": other // 2}

    def greet(k, carry):
        pl.semaphore_signal(barrier, inc=1, device_id=partner(k)[1], device_id_type=MESH)
        return carry

    lax.fori_loop(1, 64, greet, 0)
    for k in range(1, 4):
        pl.semaphore_signal(
            barrier, inc=1, device_id={"row": wrap(mx + k, 4) * 2 + ml, "col": col}, device_id_type=MESH
        )

    for b in range(4):
        first[b].wait()
        for g in range(4):
            block = jnp.concatenate([th_v[b, pl.ds(4 * g + i, 32, stride=16), :] for i in range(4)], axis=0)
            t0[g, pl.ds(b * 128, 128), :] = block.T

    sub = lax.broadcasted_iota(jnp.int32, (16, 8, 128), 1) < 4

    def blocks(f, i, value):
        value = [v.reshape(16, 8, 128) for v in value]
        rows = pl.ds(pl.multiple_of(i * 16, 16), 16)
        for g in range(2):
            left, right = value[g], value[2 + g]
            fs[f, 0, rows, pl.ds(g * 8, 8), :] = jnp.where(sub, left, pltpu.roll(right, 4, 1))
            fs[f, 1, rows, pl.ds(g * 8, 8), :] = jnp.where(sub, pltpu.roll(left, 4, 1), right)

    def theta_blocks(i, carry):
        rows = pl.ds(pl.multiple_of(i * 128, 128), 128)
        value = [t0[g, rows, :] for g in range(4)]
        blocks(0, i, value)
        for g in range(4):
            lanes = pl.ds(g * 128, 128)
            t_hl[0, rows, lanes], t_hl[1, rows, lanes] = split(value[g])
        return carry

    lax.fori_loop(0, 4, theta_blocks, 0)

    pl.semaphore_wait(barrier, 66)

    def send_fwd(f, c, velocity_part):
        mine = pl.ds(pl.multiple_of(me * 16, 16), 16)
        pltpu.make_async_copy(fs.at[f, c, me], fr.at[f, c, mine], f_recv.at[f, c]).start()

        def one(k, carry):
            other, device = partner(k)
            pltpu.make_async_remote_copy(
                src_ref=fs.at[f, c, other],
                dst_ref=fr.at[f, c, mine],
                send_sem=f_send.at[f, c],
                recv_sem=f_recv.at[f, c],
                device_id=device,
                device_id_type=MESH,
            ).start()
            return carry

        def piece(i, carry):
            lax.fori_loop(1 + 16 * i, jnp.minimum(17 + 16 * i, 64), one, 0)
            send_vel(i, velocity_part)
            return carry

        if velocity_part is None:
            lax.fori_loop(1, 64, one, 0)
        else:
            lax.fori_loop(0, 4, piece, 0)

    def send_vel(i, c):
        pltpu.make_async_remote_copy(
            src_ref=velocity.at[
                :, :, pl.ds((1 - ml) * 8 + c * 2, 2), pl.ds(pl.multiple_of(i * 128, 128), 128)
            ],
            dst_ref=vel_v.at[:, i, pl.ds(ml * 32, 32), pl.ds(c * 2, 2)],
            send_sem=vel_send.at[c],
            recv_sem=vel_recv.at[c],
            device_id={"row": mx * 2 + 1 - ml, "col": col},
            device_id_type=MESH,
        ).start()

    send_fwd(0, 0, None)

    loads[0].wait()

    def slope(i, carry):
        r = pl.multiple_of(i * 128, 128)
        value = dot3(split(mat_v[pl.ds(r, 128), :]), (t_hl[0], t_hl[1]))
        blocks(1, i, [value[:, g * 128 : g * 128 + 128] for g in range(4)])
        return carry

    lax.fori_loop(0, 4, slope, 0)
    send_fwd(1, 0, 0)
    send_fwd(0, 1, 1)
    send_fwd(1, 1, 2)
    for i in range(4):
        send_vel(i, 3)

    for copy in loads[1:]:
        copy.wait()

    def halves(i, carry):
        r = pl.multiple_of(i * 64, 64)
        tb_hl[0, pl.ds(r, 64), :], tb_hl[1, pl.ds(r, 64), :] = split(tb_v[pl.ds(r, 64), :])
        fb_hl[0, pl.ds(r, 64), :], fb_hl[1, pl.ds(r, 64), :] = split(fb_v[pl.ds(r, 64), :])
        return carry

    lax.fori_loop(0, 8, halves, 0)
    lane = lax.broadcasted_iota(jnp.int32, (1, 512), 1)
    along_wave = WAVE_ALONG * (row * 32 + lane % 32).astype(F32)
    span_id = col * 8 + (lane // 32) % 8
    span_wave = WAVE_SPAN * jnp.where(span_id < NZ // 2, span_id, span_id - NZ).astype(F32)
    waves = along_wave * along_wave + span_wave * span_wave
    for kb in range(4):
        column = jnp.broadcast_to(eig_v[:, pl.ds(kb * 128, 128)], (128, 128)).T
        for g in range(4):
            total = waves[:, g * 128 : g * 128 + 128] + column
            inv_div[pl.ds(kb * 128, 128), pl.ds(g * 128, 128)] = 1.0 / (1.0 + TIME_STEP * DIFFUSIVITY * total)
    for copy in own_vel:
        copy.wait()

    def wait_all(ref, sem):
        pltpu.make_async_copy(ref, ref, sem).wait()

    def span_stage(f, c):
        wait_all(fr.at[f, c], f_recv.at[f, c])

        def sub(i, carry):
            part = 2 * c + i

            def collect_modes(t, carry):
                start = (t % 2) * 8 + (t // 2) * 4 + 2 * i
                v = [fr[f, c, pl.ds(start + 16 * yl + j, 32, stride=32), :] for yl in range(2) for j in range(2)]
                for n, u in enumerate(regroup(v)):
                    rows = pl.ds(pl.multiple_of(t * 128 + n * 32, 32), 32)
                    x_hl[0, rows, :], x_hl[1, rows, :] = split(u)
                return carry

            lax.fori_loop(0, 4, collect_modes, 0)
            for table, h in ((span_inv, 0), (span_der, 1)) if f == 0 else ((span_inv, 2),):
                xs[part, h] = dot3((table[0], table[1]), (x_hl[0], x_hl[1]))
                mine = pl.ds(pl.multiple_of(mx * 128, 128), 128)

                def send(k, carry):
                    other = wrap(mx + k, 4)
                    pltpu.make_async_remote_copy(
                        src_ref=xs.at[part, h, pl.ds(pl.multiple_of(other * 128, 128), 128)],
                        dst_ref=xr.at[part, h, mine],
                        send_sem=x_send.at[part, h],
                        recv_sem=x_recv.at[part, h],
                        device_id={"row": other * 2 + ml, "col": col},
                        device_id_type=MESH,
                    ).start()
                    return carry

                lax.fori_loop(1, 4, send, 0)
                pltpu.make_async_copy(xs.at[part, h, mine], xr.at[part, h, mine], x_recv.at[part, h]).start()
            return carry

        lax.fori_loop(0, 2, sub, 0)

    def along_stage(part):
        flat = vel_v.reshape(3, 4, 512, 128)

        def gather_lines(n, carry):
            for h in range(3):
                v = [
                    xr[part, h, pl.ds(pl.multiple_of(n * 256 + i * 64, 64), 64), :] for i in range(4)
                ]
                for i, u in enumerate(regroup(v)):
                    yl, j = i // 2, i % 2
                    rows = pl.ds(j * 64, 64)
                    lanes = pl.ds(pl.multiple_of(n * 256 + yl * 128, 128), 128)
                    y_hl[h, 0, rows, lanes], y_hl[h, 1, rows, lanes] = split(u)
            return carry

        for h in range(3):
            wait_all(xr.at[part, h], x_recv.at[part, h])
        lax.fori_loop(0, 2, gather_lines, 0)
        wait_all(vel_v.at[:, :, pl.ds(0, 32), pl.ds(0, 2)], vel_recv.at[part])

        def product(n, carry):
            lanes = pl.ds(pl.multiple_of(n * 256, 256), 256)
            total = None
            for h, (table, component) in enumerate(((along_der, 0), (along_inv, 2), (along_inv, 1))):
                grad = dot3((y_hl[h, 0], y_hl[h, 1]), (table[0, :, lanes], table[1, :, lanes]))
                speed = jnp.concatenate(
                    [
                        jnp.concatenate(
                            [flat[component, 2 * n + b, pl.ds(2 * part + j, 64, stride=8), :] for j in range(2)], axis=0
                        )
                        for b in range(2)
                    ],
                    axis=1,
                )
                term = grad * speed
                total = term if total is None else total + term
            adv_hl[0, :, lanes], adv_hl[1, :, lanes] = split(total)
            return carry

        lax.fori_loop(0, 2, product, 0)

        def back(n, carry):
            lanes = pl.ds(pl.multiple_of(n * 256, 256), 256)
            modes = dot3((adv_hl[0], adv_hl[1]), (along_fwd[0, :, lanes], along_fwd[1, :, lanes]))
            v = [modes[j * 64 : j * 64 + 64, yl * 128 : yl * 128 + 128] for yl in range(2) for j in range(2)]
            for i, u in enumerate(regroup(v)):
                xbs[part, pl.ds(pl.multiple_of(n * 256 + i * 64, 64), 64), :] = u
            return carry

        lax.fori_loop(0, 2, back, 0)
        mine = pl.ds(pl.multiple_of(mx * 128, 128), 128)

        def send(k, carry):
            other = wrap(mx + k, 4)
            pltpu.make_async_remote_copy(
                src_ref=xbs.at[part, pl.ds(pl.multiple_of(other * 128, 128), 128)],
                dst_ref=xbr.at[part, mine],
                send_sem=xb_send.at[part],
                recv_sem=xb_recv.at[part],
                device_id={"row": other * 2 + ml, "col": col},
                device_id_type=MESH,
            ).start()
            return carry

        lax.fori_loop(1, 4, send, 0)
        pltpu.make_async_copy(xbs.at[part, mine], xbr.at[part, mine], xb_recv.at[part]).start()

    def span_back_stage(part):
        wait_all(xbr.at[part], xb_recv.at[part])
        value = dot3((span_fwd[0], span_fwd[1]), split(xbr[part]))
        real, imag = value[:256], value[256:]
        low = lax.broadcasted_iota(jnp.int32, (256, 128), 1) < 64
        bs[part, 0] = jnp.where(low, real, pltpu.roll(imag, 64, 1))
        bs[part, 1] = jnp.where(low, pltpu.roll(real, 64, 1), imag)
        mine = pl.ds(pl.multiple_of(me * 8, 8), 8)
        pltpu.make_async_copy(
            bs.at[part, ml, pl.ds(pl.multiple_of(col * 8, 8), 8)], br.at[part, mine], b_recv.at[part]
        ).start()

        def send(k, carry):
            other, device = partner(k)
            pltpu.make_async_remote_copy(
                src_ref=bs.at[part, other % 2, pl.ds(pl.multiple_of(other // 2 * 8, 8), 8)],
                dst_ref=br.at[part, mine],
                send_sem=b_send.at[part],
                recv_sem=b_recv.at[part],
                device_id=device,
                device_id_type=MESH,
            ).start()
            return carry

        lax.fori_loop(1, 64, send, 0)

    def collect(part):
        wait_all(br.at[part], b_recv.at[part])
        for n in range(2):
            v = [br[part, pl.ds(4 * n + i, 64, stride=8), :] for i in range(4)]
            for i, u in enumerate(regroup(v)):
                rows = pl.ds(2 * part + i % 2, 64, stride=8)
                g = i // 2 * 2 + n
                t0[g, rows, :] = t0[g, rows, :] + u

    span_stage(0, 0)
    span_stage(1, 0)
    along_stage(0)
    along_stage(1)
    span_back_stage(0)
    span_stage(0, 1)
    span_back_stage(1)
    span_stage(1, 1)
    along_stage(2)
    collect(0)
    along_stage(3)
    span_back_stage(2)
    collect(1)
    span_back_stage(3)
    collect(2)
    collect(3)

    def halve_right(i, carry):
        rows = pl.ds(pl.multiple_of(i * 64, 64), 64)
        for g in range(4):
            lanes = pl.ds(g * 128, 128)
            t_hl[0, rows, lanes], t_hl[1, rows, lanes] = split(t0[g, rows, :])
        return carry

    lax.fori_loop(0, 8, halve_right, 0)

    def basis(i, carry):
        rows = pl.ds(pl.multiple_of(i * 128, 128), 128)
        value = dot3((tb_hl[0, rows, :], tb_hl[1, rows, :]), (t_hl[0], t_hl[1])) * inv_div[rows, :]
        for g in range(4):
            turned = value[:, g * 128 : g * 128 + 128].T
            c_hl[0, pl.ds(g * 128, 128), rows], c_hl[1, pl.ds(g * 128, 128), rows] = split(turned)
        return carry

    lax.fori_loop(0, 4, basis, 0)

    def last(g, carry):
        rows = pl.ds(pl.multiple_of(g * 128, 128), 128)
        value = dot3(
            (c_hl[0, rows, :], c_hl[1, rows, :]), (fb_hl[0], fb_hl[1]), (((1,), (1,)), ((), ()))
        )
        for i in range(4):
            for b in range(4):
                ov[b, pl.ds(4 * g + i, 32, stride=16), :] = value[i * 32 : i * 32 + 32, b * 128 : b * 128 + 128]
        return carry

    lax.fori_loop(0, 4, last, 0)
    results = [pltpu.make_async_copy(ov.at[b], out.at[:, pl.ds(b * 128, 128)], out_sem.at[b]) for b in range(4)]
    for result in results:
        result.start()

    for c in range(2):
        for f in range(2):
            wait_all(fs.at[f, c, pl.ds(0, 63)], f_send.at[f, c])
    for part in range(4):
        wait_all(vel_v.at[:, :, pl.ds(0, 32), pl.ds(0, 2)], vel_send.at[part])
        for h in range(3):
            wait_all(xs.at[part, h, pl.ds(0, 384)], x_send.at[part, h])
        wait_all(xbs.at[part, pl.ds(0, 384)], xb_send.at[part])
        wait_all(br.at[part, pl.ds(0, 504)], b_send.at[part])
    for result in results:
        result.wait()


def shards(theta_hat, velocity, wall_derivative, to_basis, from_basis, eigenvalues):
    tables = span_tables() + along_tables()
    tables = [jnp.asarray(t) for t in tables]
    vm = pltpu.VMEM
    table = vm((2, 512, 512), BF16)
    square = vm((512, 512), F32)
    blocked = vm((4, 512, 128), F32)
    dma = pltpu.SemaphoreType.DMA
    result = pl.pallas_call(
        kernel,
        out_shape=jax.ShapeDtypeStruct((512, 512), F32),
        in_specs=[pl.BlockSpec(memory_space=pl.ANY)] * 12,
        out_specs=pl.BlockSpec(memory_space=pl.ANY),
        scratch_shapes=[
            blocked, blocked, square, square, square, vm((1, 512), F32), vm((3, 4, 64, 8, 128), F32),
            table, table, table, table, table, table,
            table, table, table, table, square,
            vm((2, 2, 64, 16, 128), F32),
            vm((2, 2, 1024, 128), F32),
            vm((2, 512, 128), BF16),
            vm((4, 3, 512, 128), F32),
            vm((4, 3, 512, 128), F32),
            vm((3, 2, 128, 512), BF16),
            vm((2, 128, 512), BF16),
            vm((4, 512, 128), F32),
            vm((4, 512, 128), F32),
            vm((4, 2, 256, 128), F32),
            vm((4, 512, 128), F32),
            table,
            blocked,
            dma((18,)), dma((4,)), dma((4,)), dma((2, 2)), dma((2, 2)), dma((4, 3)), dma((4, 3)),
            dma((4,)), dma((4,)), dma((4,)), dma((4,)), dma((4,)),
        ],
        compiler_params=pltpu.CompilerParams(
            collective_id=0, has_side_effects=True, vmem_limit_bytes=VMEM_LIMIT
        ),
        cost_estimate=pl.CostEstimate(flops=8 * 10**9, bytes_accessed=16 * 2**20, transcendentals=0),
    )(
        theta_hat.reshape(512, 512), velocity, wall_derivative, to_basis, from_basis,
        eigenvalues.reshape(1, 512), *tables,
    )
    return result.reshape(32, 2, 8, 512)


def solution(mesh):
    return jax.shard_map(
        shards,
        mesh=mesh,
        in_specs=(P("row", None, "col", None), P(None, "row", "col", None), P(), P(), P(), P()),
        out_specs=P("row", None, "col", None),
        check_vma=False,
    )
```

```python
import math

import jax
import jax.numpy as jnp
import ml_dtypes
import numpy as np
from jax import lax
from jax.experimental import pallas as pl
from jax.experimental.pallas import tpu as pltpu
from jax.sharding import PartitionSpec as P

NX = 512
NY = 512
NZ = 256
KX = 256
WAVE_ALONG = 0.01
WAVE_SPAN = 0.02
TIME_STEP = 0.25
DIFFUSIVITY = 2.0

F32 = jnp.float32
BF16 = jnp.bfloat16
MESH = pl.DeviceIdType.MESH
VMEM_LIMIT = 60 * 1024 * 1024


def split_table(table):
    table = table.astype(np.float32)
    high = table.astype(ml_dtypes.bfloat16)
    low = (table - high.astype(np.float32)).astype(ml_dtypes.bfloat16)
    return np.stack([high, low])


def span_tables():
    z = np.arange(NZ).reshape(4, 1, 64, 1, 1, 1)
    d = np.arange(2).reshape(1, 2, 1, 1, 1, 1)
    c = np.arange(2).reshape(1, 1, 1, 2, 1, 1)
    q = np.arange(NZ).reshape(32, 8).T.reshape(1, 1, 1, 1, 8, 32)
    angle = 2.0 * math.pi * ((z * q) % NZ) / NZ
    signed = WAVE_SPAN * np.where(q < NZ // 2, q, q - NZ)
    factor = 1.0 / math.sqrt(NZ)
    inverse = factor * np.cos(angle + 0.5 * math.pi * (c - d))
    derive = factor * signed * np.cos(angle + 0.5 * math.pi * (c + 1 - d))
    q = np.arange(NZ).reshape(1, 32, 8, 1, 1, 1)
    d = np.arange(2).reshape(2, 1, 1, 1, 1, 1)
    z = np.arange(NZ).reshape(1, 1, 1, 4, 1, 64)
    c = np.arange(2).reshape(1, 1, 1, 1, 2, 1)
    angle = -2.0 * math.pi * ((z * q) % NZ) / NZ
    forward = -TIME_STEP * factor * np.cos(angle + 0.5 * math.pi * (c - d))
    return [split_table(t.reshape(512, 512)) for t in (inverse, derive, forward)]


def along_tables():
    p = np.arange(KX).reshape(2, 2, 2, 1, 32, 1).transpose(0, 2, 1, 3, 4, 5)
    d = np.arange(2).reshape(1, 1, 1, 2, 1, 1)
    x = np.arange(NX).reshape(1, 1, 1, 1, 1, NX)
    angle = 2.0 * math.pi * ((p * x) % NX) / NX
    factor = math.sqrt(2.0 / NX)
    inverse = (factor * np.cos(angle + 0.5 * math.pi * d)).reshape(512, 512)
    derive = (factor * WAVE_ALONG * p * np.cos(angle + 0.5 * math.pi * (d + 1))).reshape(512, 512)
    return [split_table(t) for t in (inverse, derive, inverse.T)]


def split(value):
    high = value.astype(BF16)
    return high, (value - high.astype(F32)).astype(BF16)


def dot3(a, b, dims=(((1,), (0,)), ((), ()))):
    def one(u, v):
        return lax.dot_general(u, v, dims, preferred_element_type=F32)

    return one(a[0], b[0]) + (one(a[0], b[1]) + one(a[1], b[0]))


def regroup(v):
    lane = lax.broadcasted_iota(jnp.int32, v[0].shape, 1)
    low = lane < 64
    odd = (lane // 32) % 2 == 1
    a0 = jnp.where(low, v[0], pltpu.roll(v[2], 64, 1))
    a2 = jnp.where(low, pltpu.roll(v[0], 64, 1), v[2])
    a1 = jnp.where(low, v[1], pltpu.roll(v[3], 64, 1))
    a3 = jnp.where(low, pltpu.roll(v[1], 64, 1), v[3])
    return (
        jnp.where(odd, pltpu.roll(a1, 32, 1), a0),
        jnp.where(odd, a1, pltpu.roll(a0, 96, 1)),
        jnp.where(odd, pltpu.roll(a3, 32, 1), a2),
        jnp.where(odd, a3, pltpu.roll(a2, 96, 1)),
    )


LAST = (((1,), (1,)), ((), ()))


def wrap(value, n):
    return jnp.where(value >= n, value - n, value)


def kernel(
    theta, velocity, wall, to_basis, from_basis, eig,
    span_inv_h, span_der_h, span_fwd_h, along_inv_h, along_der_h, along_fwd_h,
    out,
    th_v, t0, mat_v, tb_v, fb_v, eig_v, vel_v,
    span_inv, span_der, span_fwd, along_inv, along_der, along_fwd,
    d_hl, t_hl, tb_hl, fb_hl, inv_div,
    fs, fr, x_hl, xs, xr, y_hl, grad, adv_hl, xbs, xbr, bs, br, c_hl, r_v, perm, tbp_hl, acc, ov,
    load_sem, vel_send, vel_recv, f_send, f_recv, x_send, x_recv, xb_send, xb_recv, b_send, b_recv, out_sem,
):
    row = lax.axis_index("row")
    col = lax.axis_index("col")
    mx = lax.div(row, 2)
    ml = lax.rem(row, 2)
    me = col * 2 + ml

    loads = [
        pltpu.make_async_copy(s, d, load_sem.at[i])
        for i, (s, d) in enumerate(
            [
                (wall, mat_v), (span_inv_h, span_inv), (span_der_h, span_der),
                (along_inv_h, along_inv), (along_der_h, along_der), (along_fwd_h, along_fwd),
                (span_fwd_h, span_fwd), (to_basis, tb_v), (from_basis, fb_v), (eig, eig_v),
            ]
        )
    ]
    first = [
        pltpu.make_async_copy(theta.at[:, pl.ds(b * 128, 128)], th_v.at[b], load_sem.at[10 + b]) for b in range(4)
    ]
    own_vel = [
        pltpu.make_async_copy(
            velocity.at[:, :, pl.ds(pl.multiple_of(ml * 8, 8), 8), pl.ds(b * 128, 128)],
            vel_v.at[:, b, pl.ds(ml * 32, 32)],
            load_sem.at[14 + b],
        )
        for b in range(4)
    ]
    for copy in first + loads + own_vel:
        copy.start()

    barrier = pltpu.get_barrier_semaphore()

    def partner(k):
        other = wrap(me + k, 64)
        return other, {"row": mx * 2 + lax.rem(other, 2), "col": lax.div(other, 2)}

    def greet(k, carry):
        pl.semaphore_signal(barrier, inc=1, device_id=partner(k)[1], device_id_type=MESH)
        return carry

    lax.fori_loop(1, 64, greet, 0)
    for k in range(1, 4):
        pl.semaphore_signal(
            barrier, inc=1, device_id={"row": wrap(mx + k, 4) * 2 + ml, "col": col}, device_id_type=MESH
        )

    for b in range(4):
        first[b].wait()
        for g in range(4):
            block = jnp.concatenate([th_v[b, pl.ds(4 * g + i, 32, stride=16), :] for i in range(4)], axis=0)
            t0[g, pl.ds(b * 128, 128), :] = block.T

    sub = lax.broadcasted_iota(jnp.int32, (16, 8, 128), 1) < 4

    def blocks(f, i, value):
        value = [v.reshape(16, 8, 128) for v in value]
        rows = pl.ds(pl.multiple_of(i * 16, 16), 16)
        for g in range(2):
            left, right = value[g], value[2 + g]
            fs[f, 0, rows, pl.ds(g * 8, 8), :] = jnp.where(sub, left, pltpu.roll(right, 4, 1))
            fs[f, 1, rows, pl.ds(g * 8, 8), :] = jnp.where(sub, pltpu.roll(left, 4, 1), right)

    def theta_blocks(i, carry):
        rows = pl.ds(pl.multiple_of(i * 128, 128), 128)
        value = [t0[g, rows, :] for g in range(4)]
        blocks(0, i, value)
        for g in range(4):
            lanes = pl.ds(g * 128, 128)
            t_hl[0, rows, lanes], t_hl[1, rows, lanes] = split(value[g])
        return carry

    lax.fori_loop(0, 4, theta_blocks, 0)

    pl.semaphore_wait(barrier, 66)

    def send_fwd(f, c, velocity_part):
        mine = pl.ds(pl.multiple_of(me * 16, 16), 16)
        pltpu.make_async_copy(fs.at[f, c, me], fr.at[f, c, mine], f_recv.at[f, c]).start()

        def one(k, carry):
            other, device = partner(k)
            pltpu.make_async_remote_copy(
                src_ref=fs.at[f, c, other],
                dst_ref=fr.at[f, c, mine],
                send_sem=f_send.at[f, c],
                recv_sem=f_recv.at[f, c],
                device_id=device,
                device_id_type=MESH,
            ).start()
            return carry

        def piece(i, carry):
            lax.fori_loop(1 + 16 * i, jnp.minimum(17 + 16 * i, 64), one, 0)
            send_vel(i, velocity_part)
            return carry

        if velocity_part is None:
            lax.fori_loop(1, 64, one, 0, unroll=7)
        else:
            lax.fori_loop(0, 4, piece, 0)

    def send_vel(i, c):
        pltpu.make_async_remote_copy(
            src_ref=velocity.at[
                :, :, pl.ds((1 - ml) * 8 + c * 2, 2), pl.ds(pl.multiple_of(i * 128, 128), 128)
            ],
            dst_ref=vel_v.at[:, i, pl.ds(ml * 32, 32), pl.ds(c * 2, 2)],
            send_sem=vel_send.at[c],
            recv_sem=vel_recv.at[c],
            device_id={"row": mx * 2 + 1 - ml, "col": col},
            device_id_type=MESH,
        ).start()

    send_fwd(0, 0, None)

    loads[0].wait()

    def slope(i, carry):
        r = pl.multiple_of(i * 128, 128)
        value = dot3(split(mat_v[pl.ds(r, 128), :]), (t_hl[0], t_hl[1]))
        blocks(1, i, [value[:, g * 128 : g * 128 + 128] for g in range(4)])
        return carry

    lax.fori_loop(0, 4, slope, 0)
    send_fwd(1, 0, 0)
    send_fwd(0, 1, 1)

    def prepare_basis():
        def halves(i, carry):
            rows = pl.ds(pl.multiple_of(i * 64, 64), 64)
            tb_hl[0, rows, :], tb_hl[1, rows, :] = split(tb_v[rows, :])
            fb_hl[0, rows, :], fb_hl[1, rows, :] = split(fb_v[rows, :])
            j = lax.broadcasted_iota(jnp.int32, (64, 512), 0) + i * 64
            n = lax.broadcasted_iota(jnp.int32, (64, 512), 1)
            perm[rows, :] = jnp.where(j == n % 64 * 8 + n // 64, 1.0, 0.0).astype(BF16)
            return carry

        lax.fori_loop(0, 8, halves, 0)
        for i in range(2):
            tbp_hl[i] = jnp.dot(tb_hl[i], perm[...], preferred_element_type=F32).astype(BF16)

    def prepare_divisor():
        def divisor(i, carry):
            rows = pl.ds(pl.multiple_of(i * 128, 128), 128)
            r = lax.broadcasted_iota(jnp.int32, (128, 512), 0) + i * 128
            along_wave = WAVE_ALONG * (row * 32 + r // 16).astype(F32)
            span_id = col * 8 + r % 8
            span_wave = WAVE_SPAN * jnp.where(span_id < NZ // 2, span_id, span_id - NZ).astype(F32)
            total = along_wave * along_wave + span_wave * span_wave + eig_v[...]
            inv_div[rows, :] = 1.0 / (1.0 + TIME_STEP * DIFFUSIVITY * total)
            for b in range(4):
                lanes = pl.ds(b * 128, 128)
                c_hl[0, rows, lanes], c_hl[1, rows, lanes] = split(th_v[b, rows, :])
            return carry

        lax.fori_loop(0, 4, divisor, 0)

    def prepare_theta():
        acc[...] = dot3((c_hl[0], c_hl[1]), (tb_hl[0], tb_hl[1]), LAST)

    def wait_all(ref, sem):
        pltpu.make_async_copy(ref, ref, sem).wait()

    def span_stage(f, c):
        wait_all(fr.at[f, c], f_recv.at[f, c])

        def sub(i, carry):
            part = 2 * c + i

            def collect_modes(t, carry):
                start = (t % 2) * 8 + (t // 2) * 4 + 2 * i
                v = [fr[f, c, pl.ds(start + 16 * yl + j, 32, stride=32), :] for yl in range(2) for j in range(2)]
                for n, u in enumerate(regroup(v)):
                    rows = pl.ds(pl.multiple_of(t * 128 + n * 32, 32), 32)
                    x_hl[0, rows, :], x_hl[1, rows, :] = split(u)
                return carry

            lax.fori_loop(0, 4, collect_modes, 0)
            for table, h in ((span_inv, 0), (span_der, 1)) if f == 0 else ((span_inv, 2),):
                xs[part, h] = dot3((table[0], table[1]), (x_hl[0], x_hl[1]))
                mine = pl.ds(pl.multiple_of(mx * 128, 128), 128)

                def send(k, carry):
                    other = wrap(mx + k, 4)
                    pltpu.make_async_remote_copy(
                        src_ref=xs.at[part, h, pl.ds(pl.multiple_of(other * 128, 128), 128)],
                        dst_ref=xr.at[part, h, mine],
                        send_sem=x_send.at[part, h],
                        recv_sem=x_recv.at[part, h],
                        device_id={"row": other * 2 + ml, "col": col},
                        device_id_type=MESH,
                    ).start()
                    return carry

                lax.fori_loop(1, 4, send, 0)
                pltpu.make_async_copy(xs.at[part, h, mine], xr.at[part, h, mine], x_recv.at[part, h]).start()
            return carry

        lax.fori_loop(0, 2, sub, 0)

    def gradient_stage(part):
        def gather_lines(n, carry):
            for h in range(3):
                v = [
                    xr[part, h, pl.ds(pl.multiple_of(n * 256 + i * 64, 64), 64), :] for i in range(4)
                ]
                for i, u in enumerate(regroup(v)):
                    yl, j = i // 2, i % 2
                    rows = pl.ds(j * 64, 64)
                    lanes = pl.ds(pl.multiple_of(n * 256 + yl * 128, 128), 128)
                    y_hl[h, 0, rows, lanes], y_hl[h, 1, rows, lanes] = split(u)
            return carry

        for h in range(3):
            wait_all(xr.at[part, h], x_recv.at[part, h])
        lax.fori_loop(0, 2, gather_lines, 0)
        for h, table in enumerate((along_der, along_inv, along_inv)):
            grad[part % 2, h] = dot3((y_hl[h, 0], y_hl[h, 1]), (table[0], table[1]))

    def along_stage(part):
        flat = vel_v.reshape(3, 4, 512, 128)
        wait_all(vel_v.at[:, :, pl.ds(0, 32), pl.ds(0, 2)], vel_recv.at[part])

        def product(b, carry):
            lanes = pl.ds(pl.multiple_of(b * 128, 128), 128)
            for j in range(2):
                rows = pl.ds(j * 64, 64)
                points = pl.ds(2 * part + j, 64, stride=8)
                total = (
                    grad[part % 2, 0, rows, lanes] * flat[0, b, points, :]
                    + grad[part % 2, 2, rows, lanes] * flat[1, b, points, :]
                    + grad[part % 2, 1, rows, lanes] * flat[2, b, points, :]
                )
                adv_hl[0, rows, lanes], adv_hl[1, rows, lanes] = split(total)
            return carry

        lax.fori_loop(0, 4, product, 0)

        def back(n, carry):
            lanes = pl.ds(pl.multiple_of(n * 256, 256), 256)
            modes = dot3((adv_hl[0], adv_hl[1]), (along_fwd[0, :, lanes], along_fwd[1, :, lanes]))
            v = [modes[j * 64 : j * 64 + 64, yl * 128 : yl * 128 + 128] for yl in range(2) for j in range(2)]
            for i, u in enumerate(regroup(v)):
                xbs[part, pl.ds(pl.multiple_of(n * 256 + i * 64, 64), 64), :] = u
            return carry

        lax.fori_loop(0, 2, back, 0)
        mine = pl.ds(pl.multiple_of(mx * 128, 128), 128)

        def send(k, carry):
            other = wrap(mx + k, 4)
            pltpu.make_async_remote_copy(
                src_ref=xbs.at[part, pl.ds(pl.multiple_of(other * 128, 128), 128)],
                dst_ref=xbr.at[part, mine],
                send_sem=xb_send.at[part],
                recv_sem=xb_recv.at[part],
                device_id={"row": other * 2 + ml, "col": col},
                device_id_type=MESH,
            ).start()
            return carry

        lax.fori_loop(1, 4, send, 0)
        pltpu.make_async_copy(xbs.at[part, mine], xbr.at[part, mine], xb_recv.at[part]).start()

    def span_back_stage(part):
        wait_all(xbr.at[part], xb_recv.at[part])
        value = dot3((span_fwd[0], span_fwd[1]), split(xbr[part]))
        real, imag = value[:256], value[256:]
        low = lax.broadcasted_iota(jnp.int32, (256, 128), 1) < 64
        bs[part, 0] = jnp.where(low, real, pltpu.roll(imag, 64, 1))
        bs[part, 1] = jnp.where(low, pltpu.roll(real, 64, 1), imag)
        mine = pl.ds(pl.multiple_of(me * 8, 8), 8)
        pltpu.make_async_copy(
            bs.at[part, ml, pl.ds(pl.multiple_of(col * 8, 8), 8)], br.at[part, mine], b_recv.at[part]
        ).start()

        def send(k, carry):
            other, device = partner(k)
            pltpu.make_async_remote_copy(
                src_ref=bs.at[part, lax.rem(other, 2), pl.ds(pl.multiple_of(lax.div(other, 2) * 8, 8), 8)],
                dst_ref=br.at[part, mine],
                send_sem=b_send.at[part],
                recv_sem=b_recv.at[part],
                device_id=device,
                device_id_type=MESH,
            ).start()
            return carry

        lax.fori_loop(1, 64, send, 0, unroll=7)

    def collect(part):
        wait_all(br.at[part], b_recv.at[part])
        for n in range(2):
            v = [br[part, pl.ds(4 * n + i, 64, stride=8), :] for i in range(4)]
            u = regroup(v)
            for c in range(2):
                turned = jnp.concatenate([u[2 * c], u[2 * c + 1]], axis=0).T
                for i in range(4):
                    r_v[pl.ds(8 * c + 4 * n + i, 32, stride=16), :] = turned[i * 32 : i * 32 + 32]
        lanes = pl.ds(part * 128, 128)
        return acc[...] + dot3(split(r_v[...]), (tbp_hl[0, :, lanes], tbp_hl[1, :, lanes]), LAST)

    for copy in loads[1:6]:
        copy.wait()
    span_stage(0, 0)
    send_fwd(1, 1, 2)
    for i in range(4):
        send_vel(i, 3)
    for copy in loads[6:] + own_vel:
        copy.wait()
    prepare_basis()
    span_stage(1, 0)
    prepare_divisor()
    gradient_stage(0)
    along_stage(0)
    gradient_stage(1)
    along_stage(1)
    prepare_theta()
    span_stage(0, 1)
    span_back_stage(0)
    span_back_stage(1)
    span_stage(1, 1)
    gradient_stage(2)
    along_stage(2)
    gradient_stage(3)
    along_stage(3)
    span_back_stage(2)
    span_back_stage(3)
    acc[...] = collect(0)
    acc[...] = collect(1)
    acc[...] = collect(2)
    c_hl[0], c_hl[1] = split(collect(3) * inv_div[...])
    results = []
    for half in range(2):
        points = pl.ds(half * 256, 256)
        ov[:, points] = dot3((c_hl[0], c_hl[1]), (fb_hl[0, points, :], fb_hl[1, points, :]), LAST)
        results.append(pltpu.make_async_copy(ov.at[:, points], out.at[:, points], out_sem.at[half]))
        results[-1].start()

    for c in range(2):
        for f in range(2):
            wait_all(fs.at[f, c, pl.ds(0, 63)], f_send.at[f, c])
    for part in range(4):
        wait_all(vel_v.at[:, :, pl.ds(0, 32), pl.ds(0, 2)], vel_send.at[part])
        for h in range(3):
            wait_all(xs.at[part, h, pl.ds(0, 384)], x_send.at[part, h])
        wait_all(xbs.at[part, pl.ds(0, 384)], xb_send.at[part])
        wait_all(br.at[part, pl.ds(0, 504)], b_send.at[part])
    for result in results:
        result.wait()


def shards(theta_hat, velocity, wall_derivative, to_basis, from_basis, eigenvalues):
    tables = span_tables() + along_tables()
    tables = [jnp.asarray(t) for t in tables]
    vm = pltpu.VMEM
    table = vm((2, 512, 512), BF16)
    square = vm((512, 512), F32)
    blocked = vm((4, 512, 128), F32)
    dma = pltpu.SemaphoreType.DMA
    result = pl.pallas_call(
        kernel,
        out_shape=jax.ShapeDtypeStruct((512, 512), F32),
        in_specs=[pl.BlockSpec(memory_space=pl.ANY)] * 12,
        out_specs=pl.BlockSpec(memory_space=pl.ANY),
        scratch_shapes=[
            blocked, blocked, square, square, square, vm((1, 512), F32), vm((3, 4, 64, 8, 128), F32),
            table, table, table, table, table, table,
            table, table, table, table, square,
            vm((2, 2, 64, 16, 128), F32),
            vm((2, 2, 1024, 128), F32),
            vm((2, 512, 128), BF16),
            vm((4, 3, 512, 128), F32),
            vm((4, 3, 512, 128), F32),
            vm((3, 2, 128, 512), BF16),
            vm((2, 3, 128, 512), F32),
            vm((2, 128, 512), BF16),
            vm((4, 512, 128), F32),
            vm((4, 512, 128), F32),
            vm((4, 2, 256, 128), F32),
            vm((4, 512, 128), F32),
            table,
            vm((512, 128), F32),
            vm((512, 512), BF16),
            table,
            square,
            square,
            dma((18,)), dma((4,)), dma((4,)), dma((2, 2)), dma((2, 2)), dma((4, 3)), dma((4, 3)),
            dma((4,)), dma((4,)), dma((4,)), dma((4,)), dma((4,)),
        ],
        compiler_params=pltpu.CompilerParams(
            collective_id=0, has_side_effects=True, vmem_limit_bytes=VMEM_LIMIT
        ),
        cost_estimate=pl.CostEstimate(flops=8 * 10**9, bytes_accessed=16 * 2**20, transcendentals=0),
    )(
        theta_hat.reshape(512, 512), velocity, wall_derivative, to_basis, from_basis,
        eigenvalues.reshape(1, 512), *tables,
    )
    return result.reshape(32, 2, 8, 512)


def solution(mesh):
    return jax.shard_map(
        shards,
        mesh=mesh,
        in_specs=(P("row", None, "col", None), P(None, "row", "col", None), P(), P(), P(), P()),
        out_specs=P("row", None, "col", None),
        check_vma=False,
    )
```

```python
import math

import jax
import jax.numpy as jnp
import ml_dtypes
import numpy as np
from jax import lax
from jax.experimental import pallas as pl
from jax.experimental.pallas import tpu as pltpu
from jax.sharding import PartitionSpec as P

NX = 512
NY = 512
NZ = 256
KX = 256
WAVE_ALONG = 0.01
WAVE_SPAN = 0.02
TIME_STEP = 0.25
DIFFUSIVITY = 2.0

F32 = jnp.float32
BF16 = jnp.bfloat16
MESH = pl.DeviceIdType.MESH
VMEM_LIMIT = 60 * 1024 * 1024


def split_table(table):
    table = table.astype(np.float32)
    high = table.astype(ml_dtypes.bfloat16)
    low = (table - high.astype(np.float32)).astype(ml_dtypes.bfloat16)
    return np.stack([high, low])


def span_tables():
    z = np.arange(NZ).reshape(4, 1, 64, 1, 1, 1)
    d = np.arange(2).reshape(1, 2, 1, 1, 1, 1)
    c = np.arange(2).reshape(1, 1, 1, 2, 1, 1)
    q = np.arange(NZ).reshape(32, 8).T.reshape(1, 1, 1, 1, 8, 32)
    angle = 2.0 * math.pi * ((z * q) % NZ) / NZ
    signed = WAVE_SPAN * np.where(q < NZ // 2, q, q - NZ)
    factor = 1.0 / math.sqrt(NZ)
    inverse = factor * np.cos(angle + 0.5 * math.pi * (c - d))
    derive = factor * signed * np.cos(angle + 0.5 * math.pi * (c + 1 - d))
    q = np.arange(NZ).reshape(1, 32, 8, 1, 1, 1)
    d = np.arange(2).reshape(2, 1, 1, 1, 1, 1)
    z = np.arange(NZ).reshape(1, 1, 1, 4, 1, 64)
    c = np.arange(2).reshape(1, 1, 1, 1, 2, 1)
    angle = -2.0 * math.pi * ((z * q) % NZ) / NZ
    forward = -TIME_STEP * factor * np.cos(angle + 0.5 * math.pi * (c - d))
    return [split_table(t.reshape(512, 512)) for t in (inverse, derive, forward)]


def along_tables():
    p = np.arange(KX).reshape(2, 2, 2, 1, 32, 1).transpose(0, 2, 1, 3, 4, 5)
    d = np.arange(2).reshape(1, 1, 1, 2, 1, 1)
    x = np.arange(NX).reshape(1, 1, 1, 1, 1, NX)
    angle = 2.0 * math.pi * ((p * x) % NX) / NX
    factor = math.sqrt(2.0 / NX)
    inverse = (factor * np.cos(angle + 0.5 * math.pi * d)).reshape(512, 512)
    derive = (factor * WAVE_ALONG * p * np.cos(angle + 0.5 * math.pi * (d + 1))).reshape(512, 512)
    return [split_table(t) for t in (inverse, derive, inverse.T)]


def split(value):
    high = value.astype(BF16)
    return high, (value - high.astype(F32)).astype(BF16)


def dot3(a, b, dims=(((1,), (0,)), ((), ()))):
    def one(u, v):
        return lax.dot_general(u, v, dims, preferred_element_type=F32)

    return one(a[0], b[0]) + (one(a[0], b[1]) + one(a[1], b[0]))


def regroup(v):
    lane = lax.broadcasted_iota(jnp.int32, v[0].shape, 1)
    low = lane < 64
    odd = (lane // 32) % 2 == 1
    a0 = jnp.where(low, v[0], pltpu.roll(v[2], 64, 1))
    a2 = jnp.where(low, pltpu.roll(v[0], 64, 1), v[2])
    a1 = jnp.where(low, v[1], pltpu.roll(v[3], 64, 1))
    a3 = jnp.where(low, pltpu.roll(v[1], 64, 1), v[3])
    return (
        jnp.where(odd, pltpu.roll(a1, 32, 1), a0),
        jnp.where(odd, a1, pltpu.roll(a0, 96, 1)),
        jnp.where(odd, pltpu.roll(a3, 32, 1), a2),
        jnp.where(odd, a3, pltpu.roll(a2, 96, 1)),
    )


LAST = (((1,), (1,)), ((), ()))


def wrap(value, n):
    return jnp.where(value >= n, value - n, value)


def kernel(
    theta, velocity, wall, to_basis, from_basis, eig,
    span_inv_h, span_der_h, span_fwd_h, along_inv_h, along_der_h, along_fwd_h,
    out,
    th_v, t0, mat_v, tb_v, fb_v, eig_v, vel_v,
    span_inv, span_der, span_fwd, along_inv, along_der, along_fwd,
    d_hl, t_hl, tb_hl, fb_hl, inv_div,
    fs, fr, x_hl, xs, xr, y_hl, grad, adv_hl, xbs, xbr, bs, br, c_hl, r_v, perm, tbp_hl, acc, ov,
    load_sem, vel_send, vel_recv, f_send, f_recv, x_send, x_recv, xb_send, xb_recv, b_send, b_recv, out_sem,
):
    row = lax.axis_index("row")
    col = lax.axis_index("col")
    mx = lax.div(row, 2)
    ml = lax.rem(row, 2)
    me = col * 2 + ml

    loads = [
        pltpu.make_async_copy(s, d, load_sem.at[i])
        for i, (s, d) in enumerate(
            [
                (wall, mat_v), (span_inv_h, span_inv), (span_der_h, span_der),
                (along_inv_h, along_inv), (along_der_h, along_der), (along_fwd_h, along_fwd),
                (span_fwd_h, span_fwd), (to_basis, tb_v), (from_basis, fb_v), (eig, eig_v),
            ]
        )
    ]
    first = [
        pltpu.make_async_copy(
            theta.at[:, pl.ds(b * 128, 128)], th_v.at[b, pl.ds(0, 512)], load_sem.at[10 + b]
        ) for b in range(4)
    ]
    own_vel = [
        pltpu.make_async_copy(
            velocity.at[:, :, pl.ds(pl.multiple_of(ml * 8, 8), 8), pl.ds(b * 128, 128)],
            vel_v.at[:, b, pl.ds(ml * 32, 32)],
            load_sem.at[14 + b],
        )
        for b in range(4)
    ]
    for copy in first + loads + own_vel:
        copy.start()

    barrier = pltpu.get_barrier_semaphore()

    def partner(k):
        other = wrap(me + k, 64)
        return other, {"row": mx * 2 + lax.rem(other, 2), "col": lax.div(other, 2)}

    def greet(k, carry):
        pl.semaphore_signal(barrier, inc=1, device_id=partner(k)[1], device_id_type=MESH)
        return carry

    lax.fori_loop(1, 64, greet, 0)
    for k in range(1, 4):
        pl.semaphore_signal(
            barrier, inc=1, device_id={"row": wrap(mx + k, 4) * 2 + ml, "col": col}, device_id_type=MESH
        )

    for b in range(4):
        first[b].wait()
        for g in range(4):
            block = jnp.concatenate([th_v[b, pl.ds(4 * g + i, 32, stride=16), :] for i in range(4)], axis=0)
            t0[g, pl.ds(b * 128, 128), :] = block.T

    sub = lax.broadcasted_iota(jnp.int32, (16, 8, 128), 1) < 4

    def blocks(f, i, value):
        value = [v.reshape(16, 8, 128) for v in value]
        rows = pl.ds(pl.multiple_of(i * 16, 16), 16)
        for g in range(2):
            left, right = value[g], value[2 + g]
            fs[f, 0, rows, pl.ds(g * 8, 8), :] = jnp.where(sub, left, pltpu.roll(right, 4, 1))
            fs[f, 1, rows, pl.ds(g * 8, 8), :] = jnp.where(sub, pltpu.roll(left, 4, 1), right)

    def theta_blocks(i, carry):
        rows = pl.ds(pl.multiple_of(i * 128, 128), 128)
        value = [t0[g, rows, :] for g in range(4)]
        blocks(0, i, value)
        for g in range(4):
            lanes = pl.ds(g * 128, 128)
            t_hl[0, rows, lanes], t_hl[1, rows, lanes] = split(value[g])
        return carry

    lax.fori_loop(0, 4, theta_blocks, 0)

    pl.semaphore_wait(barrier, 66)

    def send_fwd(f, c, velocity_part):
        mine = pl.ds(pl.multiple_of(me * 16, 16), 16)
        pltpu.make_async_copy(fs.at[f, c, me], fr.at[f, c, mine], f_recv.at[f, c]).start()

        def one(k, carry):
            other, device = partner(k)
            pltpu.make_async_remote_copy(
                src_ref=fs.at[f, c, other],
                dst_ref=fr.at[f, c, mine],
                send_sem=f_send.at[f, c],
                recv_sem=f_recv.at[f, c],
                device_id=device,
                device_id_type=MESH,
            ).start()
            return carry

        def piece(i, carry):
            lax.fori_loop(1 + 16 * i, jnp.minimum(17 + 16 * i, 64), one, 0)
            send_vel(i, velocity_part)
            return carry

        if velocity_part is None:
            lax.fori_loop(1, 64, one, 0, unroll=7)
        else:
            lax.fori_loop(0, 4, piece, 0)

    def send_vel(i, c):
        pltpu.make_async_remote_copy(
            src_ref=velocity.at[
                :, :, pl.ds((1 - ml) * 8 + c * 2, 2), pl.ds(pl.multiple_of(i * 128, 128), 128)
            ],
            dst_ref=vel_v.at[:, i, pl.ds(ml * 32, 32), pl.ds(c * 2, 2)],
            send_sem=vel_send.at[c],
            recv_sem=vel_recv.at[c],
            device_id={"row": mx * 2 + 1 - ml, "col": col},
            device_id_type=MESH,
        ).start()

    send_fwd(0, 0, None)

    loads[0].wait()

    def slope(i, carry):
        r = pl.multiple_of(i * 128, 128)
        value = dot3(split(mat_v[pl.ds(r, 128), :]), (t_hl[0], t_hl[1]))
        blocks(1, i, [value[:, g * 128 : g * 128 + 128] for g in range(4)])
        return carry

    lax.fori_loop(0, 4, slope, 0)
    send_fwd(1, 0, 0)
    send_fwd(0, 1, 1)

    def prepare_basis():
        def halves(i, carry):
            rows = pl.ds(pl.multiple_of(i * 64, 64), 64)
            tb_hl[0, rows, :], tb_hl[1, rows, :] = split(tb_v[rows, :])
            fb_hl[0, rows, :], fb_hl[1, rows, :] = split(fb_v[rows, :])
            j = lax.broadcasted_iota(jnp.int32, (64, 512), 0) + i * 64
            n = lax.broadcasted_iota(jnp.int32, (64, 512), 1)
            perm[rows, :] = jnp.where(j == n % 64 * 8 + n // 64, 1.0, 0.0).astype(BF16)
            return carry

        lax.fori_loop(0, 8, halves, 0)
        for i in range(2):
            tbp_hl[i] = jnp.dot(tb_hl[i], perm[...], preferred_element_type=F32).astype(BF16)

    def prepare_divisor():
        def divisor(i, carry):
            rows = pl.ds(pl.multiple_of(i * 128, 128), 128)
            r = lax.broadcasted_iota(jnp.int32, (128, 512), 0) + i * 128
            along_wave = WAVE_ALONG * (row * 32 + r // 16).astype(F32)
            span_id = col * 8 + r % 8
            span_wave = WAVE_SPAN * jnp.where(span_id < NZ // 2, span_id, span_id - NZ).astype(F32)
            total = along_wave * along_wave + span_wave * span_wave + eig_v[...]
            inv_div[rows, :] = 1.0 / (1.0 + TIME_STEP * DIFFUSIVITY * total)
            for b in range(4):
                lanes = pl.ds(b * 128, 128)
                c_hl[0, rows, lanes], c_hl[1, rows, lanes] = split(th_v[b, rows, :])
            return carry

        lax.fori_loop(0, 4, divisor, 0)

    def prepare_theta():
        acc[...] = dot3((c_hl[0], c_hl[1]), (tb_hl[0], tb_hl[1]), LAST)

    def wait_all(ref, sem):
        pltpu.make_async_copy(ref, ref, sem).wait()

    def span_stage(f, c):
        wait_all(fr.at[f, c, pl.ds(0, 1024)], f_recv.at[f, c])

        def sub(i, carry):
            part = 2 * c + i

            def collect_modes(t, carry):
                start = (t % 2) * 8 + (t // 2) * 4 + 2 * i
                v = [fr[f, c, pl.ds(start + 16 * yl + j, 32, stride=32), :] for yl in range(2) for j in range(2)]
                for n, u in enumerate(regroup(v)):
                    rows = pl.ds(pl.multiple_of(t * 128 + n * 32, 32), 32)
                    x_hl[0, rows, :], x_hl[1, rows, :] = split(u)
                return carry

            lax.fori_loop(0, 4, collect_modes, 0)
            for table, h in ((span_inv, 0), (span_der, 1)) if f == 0 else ((span_inv, 2),):
                xs[part, h] = dot3((table[0], table[1]), (x_hl[0], x_hl[1]))
                mine = pl.ds(pl.multiple_of(mx * 128, 128), 128)

                def send(k, carry):
                    other = wrap(mx + k, 4)
                    pltpu.make_async_remote_copy(
                        src_ref=xs.at[part, h, pl.ds(pl.multiple_of(other * 128, 128), 128)],
                        dst_ref=xr.at[part, h, mine],
                        send_sem=x_send.at[part, h],
                        recv_sem=x_recv.at[part, h],
                        device_id={"row": other * 2 + ml, "col": col},
                        device_id_type=MESH,
                    ).start()
                    return carry

                lax.fori_loop(1, 4, send, 0)
                pltpu.make_async_copy(xs.at[part, h, mine], xr.at[part, h, mine], x_recv.at[part, h]).start()
            return carry

        lax.fori_loop(0, 2, sub, 0)

    def gradient_stage(part):
        def gather_lines(n, carry):
            for h in range(3):
                v = [
                    xr[part, h, pl.ds(pl.multiple_of(n * 256 + i * 64, 64), 64), :] for i in range(4)
                ]
                for i, u in enumerate(regroup(v)):
                    yl, j = i // 2, i % 2
                    rows = pl.ds(j * 64, 64)
                    lanes = pl.ds(pl.multiple_of(n * 256 + yl * 128, 128), 128)
                    y_hl[h, 0, rows, lanes], y_hl[h, 1, rows, lanes] = split(u)
            return carry

        for h in range(3):
            wait_all(xr.at[part, h], x_recv.at[part, h])
        lax.fori_loop(0, 2, gather_lines, 0)
        for h, table in enumerate((along_der, along_inv, along_inv)):
            grad[part % 2, h] = dot3((y_hl[h, 0], y_hl[h, 1]), (table[0], table[1]))

    def along_stage(part):
        flat = vel_v.reshape(3, 4, 520, 128)
        wait_all(vel_v.at[:, :, pl.ds(0, 32), pl.ds(0, 2)], vel_recv.at[part])

        def product(b, carry):
            lanes = pl.ds(pl.multiple_of(b * 128, 128), 128)
            for j in range(2):
                rows = pl.ds(j * 64, 64)
                points = pl.ds(2 * part + j, 64, stride=8)
                total = (
                    grad[part % 2, 0, rows, lanes] * flat[0, b, points, :]
                    + grad[part % 2, 2, rows, lanes] * flat[1, b, points, :]
                    + grad[part % 2, 1, rows, lanes] * flat[2, b, points, :]
                )
                adv_hl[0, rows, lanes], adv_hl[1, rows, lanes] = split(total)
            return carry

        lax.fori_loop(0, 4, product, 0)

        def back(n, carry):
            lanes = pl.ds(pl.multiple_of(n * 256, 256), 256)
            modes = dot3((adv_hl[0], adv_hl[1]), (along_fwd[0, :, lanes], along_fwd[1, :, lanes]))
            v = [modes[j * 64 : j * 64 + 64, yl * 128 : yl * 128 + 128] for yl in range(2) for j in range(2)]
            for i, u in enumerate(regroup(v)):
                xbs[part, pl.ds(pl.multiple_of(n * 256 + i * 64, 64), 64), :] = u
            return carry

        lax.fori_loop(0, 2, back, 0)
        mine = pl.ds(pl.multiple_of(mx * 128, 128), 128)

        def send(k, carry):
            other = wrap(mx + k, 4)
            pltpu.make_async_remote_copy(
                src_ref=xbs.at[part, pl.ds(pl.multiple_of(other * 128, 128), 128)],
                dst_ref=xbr.at[part, mine],
                send_sem=xb_send.at[part],
                recv_sem=xb_recv.at[part],
                device_id={"row": other * 2 + ml, "col": col},
                device_id_type=MESH,
            ).start()
            return carry

        lax.fori_loop(1, 4, send, 0)
        pltpu.make_async_copy(xbs.at[part, mine], xbr.at[part, mine], xb_recv.at[part]).start()

    def span_back_stage(part):
        wait_all(xbr.at[part], xb_recv.at[part])
        value = dot3((span_fwd[0], span_fwd[1]), split(xbr[part]))
        real, imag = value[:256], value[256:]
        low = lax.broadcasted_iota(jnp.int32, (256, 128), 1) < 64
        bs[part, 0] = jnp.where(low, real, pltpu.roll(imag, 64, 1))
        bs[part, 1] = jnp.where(low, pltpu.roll(real, 64, 1), imag)
        mine = pl.ds(pl.multiple_of(me * 8, 8), 8)
        pltpu.make_async_copy(
            bs.at[part, ml, pl.ds(pl.multiple_of(col * 8, 8), 8)], br.at[part, mine], b_recv.at[part]
        ).start()

        def send(k, carry):
            other, device = partner(k)
            pltpu.make_async_remote_copy(
                src_ref=bs.at[part, lax.rem(other, 2), pl.ds(pl.multiple_of(lax.div(other, 2) * 8, 8), 8)],
                dst_ref=br.at[part, mine],
                send_sem=b_send.at[part],
                recv_sem=b_recv.at[part],
                device_id=device,
                device_id_type=MESH,
            ).start()
            return carry

        lax.fori_loop(1, 64, send, 0, unroll=7)

    def collect(part):
        wait_all(br.at[part, pl.ds(0, 512)], b_recv.at[part])
        for n in range(2):
            v = [br[part, pl.ds(4 * n + i, 64, stride=8), :] for i in range(4)]
            u = regroup(v)
            for c in range(2):
                turned = jnp.concatenate([u[2 * c], u[2 * c + 1]], axis=0).T
                for i in range(4):
                    r_v[pl.ds(8 * c + 4 * n + i, 32, stride=16), :] = turned[i * 32 : i * 32 + 32]
        lanes = pl.ds(part * 128, 128)
        return acc[...] + dot3(split(r_v[pl.ds(0, 512), :]), (tbp_hl[0, :, lanes], tbp_hl[1, :, lanes]), LAST)

    for copy in loads[1:6]:
        copy.wait()
    span_stage(0, 0)
    send_fwd(1, 1, 2)
    for i in range(4):
        send_vel(i, 3)
    for copy in loads[6:] + own_vel:
        copy.wait()
    prepare_basis()
    span_stage(1, 0)
    prepare_divisor()
    gradient_stage(0)
    along_stage(0)
    span_stage(0, 1)
    gradient_stage(1)
    along_stage(1)
    span_stage(1, 1)
    prepare_theta()
    span_back_stage(0)
    span_back_stage(1)
    gradient_stage(2)
    along_stage(2)
    gradient_stage(3)
    along_stage(3)
    span_back_stage(2)
    span_back_stage(3)
    acc[...] = collect(0)
    acc[...] = collect(1)
    acc[...] = collect(2)
    c_hl[0], c_hl[1] = split(collect(3) * inv_div[...])
    results = []
    for half in range(2):
        points = pl.ds(half * 256, 256)
        ov[:, points] = dot3((c_hl[0], c_hl[1]), (fb_hl[0, points, :], fb_hl[1, points, :]), LAST)
        results.append(pltpu.make_async_copy(ov.at[:, points], out.at[:, points], out_sem.at[half]))
        results[-1].start()

    for c in range(2):
        for f in range(2):
            wait_all(fs.at[f, c, pl.ds(0, 63)], f_send.at[f, c])
    for part in range(4):
        wait_all(vel_v.at[:, :, pl.ds(0, 32), pl.ds(0, 2)], vel_send.at[part])
        for h in range(3):
            wait_all(xs.at[part, h, pl.ds(0, 384)], x_send.at[part, h])
        wait_all(xbs.at[part, pl.ds(0, 384)], xb_send.at[part])
        wait_all(br.at[part, pl.ds(0, 504)], b_send.at[part])
    for result in results:
        result.wait()


def shards(theta_hat, velocity, wall_derivative, to_basis, from_basis, eigenvalues):
    tables = span_tables() + along_tables()
    tables = [jnp.asarray(t) for t in tables]
    vm = pltpu.VMEM
    table = vm((2, 512, 512), BF16)
    square = vm((512, 512), F32)
    blocked = vm((4, 512, 128), F32)
    dma = pltpu.SemaphoreType.DMA
    result = pl.pallas_call(
        kernel,
        out_shape=jax.ShapeDtypeStruct((512, 512), F32),
        in_specs=[pl.BlockSpec(memory_space=pl.ANY)] * 12,
        out_specs=pl.BlockSpec(memory_space=pl.ANY),
        scratch_shapes=[
            vm((4, 528, 128), F32), blocked, square, square, square, vm((1, 512), F32), vm((3, 4, 65, 8, 128), F32),
            table, table, table, table, table, table,
            table, table, table, table, square,
            vm((2, 2, 64, 16, 128), F32),
            vm((2, 2, 1056, 128), F32),
            vm((2, 512, 128), BF16),
            vm((4, 3, 512, 128), F32),
            vm((4, 3, 512, 128), F32),
            vm((3, 2, 128, 512), BF16),
            vm((2, 3, 128, 512), F32),
            vm((2, 128, 512), BF16),
            vm((4, 512, 128), F32),
            vm((4, 512, 128), F32),
            vm((4, 2, 256, 128), F32),
            vm((4, 520, 128), F32),
            table,
            vm((528, 128), F32),
            vm((512, 512), BF16),
            table,
            square,
            square,
            dma((18,)), dma((4,)), dma((4,)), dma((2, 2)), dma((2, 2)), dma((4, 3)), dma((4, 3)),
            dma((4,)), dma((4,)), dma((4,)), dma((4,)), dma((4,)),
        ],
        compiler_params=pltpu.CompilerParams(
            collective_id=0, has_side_effects=True, vmem_limit_bytes=VMEM_LIMIT
        ),
        cost_estimate=pl.CostEstimate(flops=8 * 10**9, bytes_accessed=16 * 2**20, transcendentals=0),
    )(
        theta_hat.reshape(512, 512), velocity, wall_derivative, to_basis, from_basis,
        eigenvalues.reshape(1, 512), *tables,
    )
    return result.reshape(32, 2, 8, 512)


def solution(mesh):
    return jax.shard_map(
        shards,
        mesh=mesh,
        in_specs=(P("row", None, "col", None), P(None, "row", "col", None), P(), P(), P(), P()),
        out_specs=P("row", None, "col", None),
        check_vma=False,
    )
```

```python
import math

import jax
import jax.numpy as jnp
import ml_dtypes
import numpy as np
from jax import lax
from jax.experimental import pallas as pl
from jax.experimental.pallas import tpu as pltpu
from jax.sharding import PartitionSpec as P

NX = 512
NY = 512
NZ = 256
KX = 256
WAVE_ALONG = 0.01
WAVE_SPAN = 0.02
TIME_STEP = 0.25
DIFFUSIVITY = 2.0

F32 = jnp.float32
BF16 = jnp.bfloat16
MESH = pl.DeviceIdType.MESH
VMEM_LIMIT = 60 * 1024 * 1024


def split_table(table):
    table = table.astype(np.float32)
    high = table.astype(ml_dtypes.bfloat16)
    low = (table - high.astype(np.float32)).astype(ml_dtypes.bfloat16)
    return np.stack([high, low])


def span_tables():
    z = np.arange(NZ).reshape(4, 1, 64, 1, 1, 1)
    d = np.arange(2).reshape(1, 2, 1, 1, 1, 1)
    c = np.arange(2).reshape(1, 1, 1, 2, 1, 1)
    q = np.arange(NZ).reshape(32, 8).T.reshape(1, 1, 1, 1, 8, 32)
    angle = 2.0 * math.pi * ((z * q) % NZ) / NZ
    signed = WAVE_SPAN * np.where(q < NZ // 2, q, q - NZ)
    factor = 1.0 / math.sqrt(NZ)
    inverse = factor * np.cos(angle + 0.5 * math.pi * (c - d))
    derive = factor * signed * np.cos(angle + 0.5 * math.pi * (c + 1 - d))
    q = np.arange(NZ).reshape(1, 32, 8, 1, 1, 1)
    d = np.arange(2).reshape(2, 1, 1, 1, 1, 1)
    z = np.arange(NZ).reshape(1, 1, 1, 4, 1, 64)
    c = np.arange(2).reshape(1, 1, 1, 1, 2, 1)
    angle = -2.0 * math.pi * ((z * q) % NZ) / NZ
    forward = -TIME_STEP * factor * np.cos(angle + 0.5 * math.pi * (c - d))
    return [split_table(t.reshape(512, 512)) for t in (inverse, derive, forward)]


def along_tables():
    p = np.arange(KX).reshape(2, 2, 2, 1, 32, 1).transpose(0, 2, 1, 3, 4, 5)
    d = np.arange(2).reshape(1, 1, 1, 2, 1, 1)
    x = np.arange(NX).reshape(1, 1, 1, 1, 1, NX)
    angle = 2.0 * math.pi * ((p * x) % NX) / NX
    factor = math.sqrt(2.0 / NX)
    inverse = (factor * np.cos(angle + 0.5 * math.pi * d)).reshape(512, 512)
    derive = (factor * WAVE_ALONG * p * np.cos(angle + 0.5 * math.pi * (d + 1))).reshape(512, 512)
    return [split_table(t) for t in (inverse, derive, inverse.T)]


def split(value):
    high = value.astype(BF16)
    return high, (value - high.astype(F32)).astype(BF16)


def dot3(a, b, dims=(((1,), (0,)), ((), ()))):
    def one(u, v):
        return lax.dot_general(u, v, dims, preferred_element_type=F32)

    return one(a[0], b[0]) + (one(a[0], b[1]) + one(a[1], b[0]))


def regroup(v):
    lane = lax.broadcasted_iota(jnp.int32, v[0].shape, 1)
    low = lane < 64
    odd = (lane // 32) % 2 == 1
    a0 = jnp.where(low, v[0], pltpu.roll(v[2], 64, 1))
    a2 = jnp.where(low, pltpu.roll(v[0], 64, 1), v[2])
    a1 = jnp.where(low, v[1], pltpu.roll(v[3], 64, 1))
    a3 = jnp.where(low, pltpu.roll(v[1], 64, 1), v[3])
    return (
        jnp.where(odd, pltpu.roll(a1, 32, 1), a0),
        jnp.where(odd, a1, pltpu.roll(a0, 96, 1)),
        jnp.where(odd, pltpu.roll(a3, 32, 1), a2),
        jnp.where(odd, a3, pltpu.roll(a2, 96, 1)),
    )


LAST = (((1,), (1,)), ((), ()))


def wrap(value, n):
    return jnp.where(value >= n, value - n, value)


def kernel(
    theta, velocity, wall, to_basis, from_basis, eig,
    span_inv_h, span_der_h, span_fwd_h, along_inv_h, along_der_h, along_fwd_h,
    out,
    th_v, t0, mat_v, tb_v, fb_v, eig_v, vel_v,
    span_inv, span_der, span_fwd, along_inv, along_der, along_fwd,
    d_hl, t_hl, tb_hl, fb_hl, inv_div,
    fs, fr, x_hl, xs, xr, y_hl, grad, adv_hl, xbs, xbr, bs, br, c_hl, r_v, perm, tbp_hl, acc, ov,
    load_sem, vel_send, vel_recv, f_send, f_recv, x_send, x_recv, xb_send, xb_recv, b_send, b_recv, out_sem,
):
    row = lax.axis_index("row")
    col = lax.axis_index("col")
    mx = lax.div(row, 2)
    ml = lax.rem(row, 2)
    me = col * 2 + ml

    loads = [
        pltpu.make_async_copy(s, d, load_sem.at[i])
        for i, (s, d) in enumerate(
            [
                (wall, mat_v), (span_inv_h, span_inv), (span_der_h, span_der),
                (along_inv_h, along_inv), (along_der_h, along_der), (along_fwd_h, along_fwd),
                (span_fwd_h, span_fwd), (to_basis, tb_v), (from_basis, fb_v), (eig, eig_v),
            ]
        )
    ]
    first = [
        pltpu.make_async_copy(
            theta.at[:, pl.ds(b * 128, 128)], th_v.at[b, pl.ds(0, 512)], load_sem.at[10 + b]
        ) for b in range(4)
    ]
    own_vel = [
        pltpu.make_async_copy(
            velocity.at[:, :, pl.ds(pl.multiple_of(ml * 8, 8), 8), pl.ds(b * 128, 128)],
            vel_v.at[:, b, pl.ds(ml * 32, 32)],
            load_sem.at[14 + b],
        )
        for b in range(4)
    ]
    for copy in first + loads + own_vel:
        copy.start()

    barrier = pltpu.get_barrier_semaphore()

    def partner(k):
        other = wrap(me + k, 64)
        return other, {"row": mx * 2 + lax.rem(other, 2), "col": lax.div(other, 2)}

    def greet(k, carry):
        pl.semaphore_signal(barrier, inc=1, device_id=partner(k)[1], device_id_type=MESH)
        return carry

    lax.fori_loop(1, 64, greet, 0)
    for k in range(1, 4):
        pl.semaphore_signal(
            barrier, inc=1, device_id={"row": wrap(mx + k, 4) * 2 + ml, "col": col}, device_id_type=MESH
        )

    for b in range(4):
        first[b].wait()
        for g in range(4):
            block = jnp.concatenate([th_v[b, pl.ds(4 * g + i, 32, stride=16), :] for i in range(4)], axis=0)
            t0[g, pl.ds(b * 128, 128), :] = block.T

    sub = lax.broadcasted_iota(jnp.int32, (16, 8, 128), 1) < 4

    def blocks(f, i, value):
        value = [v.reshape(16, 8, 128) for v in value]
        rows = pl.ds(pl.multiple_of(i * 16, 16), 16)
        for g in range(2):
            left, right = value[g], value[2 + g]
            fs[f, 0, rows, pl.ds(g * 8, 8), :] = jnp.where(sub, left, pltpu.roll(right, 4, 1))
            fs[f, 1, rows, pl.ds(g * 8, 8), :] = jnp.where(sub, pltpu.roll(left, 4, 1), right)

    def theta_blocks(i, carry):
        rows = pl.ds(pl.multiple_of(i * 128, 128), 128)
        value = [t0[g, rows, :] for g in range(4)]
        blocks(0, i, value)
        for g in range(4):
            lanes = pl.ds(g * 128, 128)
            t_hl[0, rows, lanes], t_hl[1, rows, lanes] = split(value[g])
        return carry

    lax.fori_loop(0, 4, theta_blocks, 0)

    pl.semaphore_wait(barrier, 66)

    def send_fwd(f, c, velocity_part):
        mine = pl.ds(pl.multiple_of(me * 16, 16), 16)
        pltpu.make_async_copy(fs.at[f, c, me], fr.at[f, c, mine], f_recv.at[f, c]).start()

        def one(k, carry):
            other, device = partner(k)
            pltpu.make_async_remote_copy(
                src_ref=fs.at[f, c, other],
                dst_ref=fr.at[f, c, mine],
                send_sem=f_send.at[f, c],
                recv_sem=f_recv.at[f, c],
                device_id=device,
                device_id_type=MESH,
            ).start()
            return carry

        def piece(i, carry):
            lax.fori_loop(1 + 16 * i, jnp.minimum(17 + 16 * i, 64), one, 0)
            send_vel(i, velocity_part)
            return carry

        if velocity_part is None:
            lax.fori_loop(1, 64, one, 0, unroll=7)
        else:
            lax.fori_loop(0, 4, piece, 0)

    def send_vel(i, c):
        pltpu.make_async_remote_copy(
            src_ref=velocity.at[
                :, :, pl.ds((1 - ml) * 8 + c * 2, 2), pl.ds(pl.multiple_of(i * 128, 128), 128)
            ],
            dst_ref=vel_v.at[:, i, pl.ds(ml * 32, 32), pl.ds(c * 2, 2)],
            send_sem=vel_send.at[c],
            recv_sem=vel_recv.at[c],
            device_id={"row": mx * 2 + 1 - ml, "col": col},
            device_id_type=MESH,
        ).start()

    send_fwd(0, 0, None)

    loads[0].wait()

    def slope(i, carry):
        r = pl.multiple_of(i * 128, 128)
        value = dot3(split(mat_v[pl.ds(r, 128), :]), (t_hl[0], t_hl[1]))
        blocks(1, i, [value[:, g * 128 : g * 128 + 128] for g in range(4)])
        return carry

    lax.fori_loop(0, 4, slope, 0)
    send_fwd(1, 0, 0)
    send_fwd(0, 1, 1)

    def prepare_basis():
        def halves(i, carry):
            rows = pl.ds(pl.multiple_of(i * 64, 64), 64)
            tb_hl[0, rows, :], tb_hl[1, rows, :] = split(tb_v[rows, :])
            fb_hl[0, rows, :], fb_hl[1, rows, :] = split(fb_v[rows, :])
            j = lax.broadcasted_iota(jnp.int32, (64, 512), 0) + i * 64
            n = lax.broadcasted_iota(jnp.int32, (64, 512), 1)
            perm[rows, :] = jnp.where(j == n % 64 * 8 + n // 64, 1.0, 0.0).astype(BF16)
            return carry

        lax.fori_loop(0, 8, halves, 0)
        for i in range(2):
            tbp_hl[i] = jnp.dot(tb_hl[i], perm[...], preferred_element_type=F32).astype(BF16)

    def prepare_divisor():
        def divisor(i, carry):
            rows = pl.ds(pl.multiple_of(i * 128, 128), 128)
            r = lax.broadcasted_iota(jnp.int32, (128, 512), 0) + i * 128
            along_wave = WAVE_ALONG * (row * 32 + r // 16).astype(F32)
            span_id = col * 8 + r % 8
            span_wave = WAVE_SPAN * jnp.where(span_id < NZ // 2, span_id, span_id - NZ).astype(F32)
            total = along_wave * along_wave + span_wave * span_wave + eig_v[...]
            inv_div[rows, :] = 1.0 / (1.0 + TIME_STEP * DIFFUSIVITY * total)
            for b in range(4):
                lanes = pl.ds(b * 128, 128)
                c_hl[0, rows, lanes], c_hl[1, rows, lanes] = split(th_v[b, rows, :])
            return carry

        lax.fori_loop(0, 4, divisor, 0)

    def prepare_theta():
        acc[...] = dot3((c_hl[0], c_hl[1]), (tb_hl[0], tb_hl[1]), LAST)

    def wait_all(ref, sem):
        pltpu.make_async_copy(ref, ref, sem).wait()

    def span_stage(f, c):
        wait_all(fr.at[f, c, pl.ds(0, 1024)], f_recv.at[f, c])

        def collect_modes(t, carry):
            start = lax.rem(t, 2) * 8 + lax.div(t, 2) * 4
            for i in range(2):
                v = [
                    fr[f, c, pl.ds(start + 2 * i + 16 * yl + j, 32, stride=32), :] for yl in range(2) for j in range(2)
                ]
                lanes = pl.ds(i * 128, 128)
                for n, u in enumerate(regroup(v)):
                    rows = pl.ds(pl.multiple_of(t * 128 + n * 32, 32), 32)
                    x_hl[0, rows, lanes], x_hl[1, rows, lanes] = split(u)
            return carry

        lax.fori_loop(0, 4, collect_modes, 0)
        mine = pl.ds(pl.multiple_of(mx * 128, 128), 128)
        for table, h in ((span_inv, 0), (span_der, 1)) if f == 0 else ((span_inv, 2),):
            value = dot3((table[0], table[1]), (x_hl[0], x_hl[1]))
            for i in range(2):
                xs[2 * c + i, h] = value[:, i * 128 : i * 128 + 128]
            for part in (2 * c, 2 * c + 1):

                def send(k, carry):
                    other = wrap(mx + k, 4)
                    pltpu.make_async_remote_copy(
                        src_ref=xs.at[part, h, pl.ds(pl.multiple_of(other * 128, 128), 128)],
                        dst_ref=xr.at[part, h, mine],
                        send_sem=x_send.at[part, h],
                        recv_sem=x_recv.at[part, h],
                        device_id={"row": other * 2 + ml, "col": col},
                        device_id_type=MESH,
                    ).start()
                    return carry

                lax.fori_loop(1, 4, send, 0)
                pltpu.make_async_copy(xs.at[part, h, mine], xr.at[part, h, mine], x_recv.at[part, h]).start()

    def gradient_stage(part):
        def gather_lines(n, carry):
            for h in range(3):
                v = [
                    xr[part, h, pl.ds(pl.multiple_of(n * 256 + i * 64, 64), 64), :] for i in range(4)
                ]
                for i, u in enumerate(regroup(v)):
                    yl, j = i // 2, i % 2
                    rows = pl.ds(j * 64, 64)
                    lanes = pl.ds(pl.multiple_of(n * 256 + yl * 128, 128), 128)
                    y_hl[h, 0, rows, lanes], y_hl[h, 1, rows, lanes] = split(u)
            return carry

        for h in range(3):
            wait_all(xr.at[part, h], x_recv.at[part, h])
        lax.fori_loop(0, 2, gather_lines, 0)
        for h, table in enumerate((along_der, along_inv, along_inv)):
            grad[part % 2, h] = dot3((y_hl[h, 0], y_hl[h, 1]), (table[0], table[1]))

    def along_stage(part):
        flat = vel_v.reshape(3, 4, 520, 128)
        wait_all(vel_v.at[:, :, pl.ds(0, 32), pl.ds(0, 2)], vel_recv.at[part])

        def product(b, carry):
            lanes = pl.ds(pl.multiple_of(b * 128, 128), 128)
            for j in range(2):
                rows = pl.ds(j * 64, 64)
                points = pl.ds(2 * part + j, 64, stride=8)
                total = (
                    grad[part % 2, 0, rows, lanes] * flat[0, b, points, :]
                    + grad[part % 2, 2, rows, lanes] * flat[1, b, points, :]
                    + grad[part % 2, 1, rows, lanes] * flat[2, b, points, :]
                )
                adv_hl[0, rows, lanes], adv_hl[1, rows, lanes] = split(total)
            return carry

        lax.fori_loop(0, 4, product, 0)

        def back(n, carry):
            lanes = pl.ds(pl.multiple_of(n * 256, 256), 256)
            modes = dot3((adv_hl[0], adv_hl[1]), (along_fwd[0, :, lanes], along_fwd[1, :, lanes]))
            v = [modes[j * 64 : j * 64 + 64, yl * 128 : yl * 128 + 128] for yl in range(2) for j in range(2)]
            for i, u in enumerate(regroup(v)):
                xbs[part, pl.ds(pl.multiple_of(n * 256 + i * 64, 64), 64), :] = u
            return carry

        lax.fori_loop(0, 2, back, 0)
        mine = pl.ds(pl.multiple_of(mx * 128, 128), 128)

        def send(k, carry):
            other = wrap(mx + k, 4)
            pltpu.make_async_remote_copy(
                src_ref=xbs.at[part, pl.ds(pl.multiple_of(other * 128, 128), 128)],
                dst_ref=xbr.at[part, mine],
                send_sem=xb_send.at[part],
                recv_sem=xb_recv.at[part],
                device_id={"row": other * 2 + ml, "col": col},
                device_id_type=MESH,
            ).start()
            return carry

        lax.fori_loop(1, 4, send, 0)
        pltpu.make_async_copy(xbs.at[part, mine], xbr.at[part, mine], xb_recv.at[part]).start()

    def span_back_stage(part):
        wait_all(xbr.at[part], xb_recv.at[part])
        value = dot3((span_fwd[0], span_fwd[1]), split(xbr[part]))
        real, imag = value[:256], value[256:]
        low = lax.broadcasted_iota(jnp.int32, (256, 128), 1) < 64
        bs[part, 0] = jnp.where(low, real, pltpu.roll(imag, 64, 1))
        bs[part, 1] = jnp.where(low, pltpu.roll(real, 64, 1), imag)
        mine = pl.ds(pl.multiple_of(me * 8, 8), 8)
        pltpu.make_async_copy(
            bs.at[part, ml, pl.ds(pl.multiple_of(col * 8, 8), 8)], br.at[part, mine], b_recv.at[part]
        ).start()

        def send(k, carry):
            other, device = partner(k)
            pltpu.make_async_remote_copy(
                src_ref=bs.at[part, lax.rem(other, 2), pl.ds(pl.multiple_of(lax.div(other, 2) * 8, 8), 8)],
                dst_ref=br.at[part, mine],
                send_sem=b_send.at[part],
                recv_sem=b_recv.at[part],
                device_id=device,
                device_id_type=MESH,
            ).start()
            return carry

        lax.fori_loop(1, 64, send, 0, unroll=7)

    def collect(part):
        wait_all(br.at[part, pl.ds(0, 512)], b_recv.at[part])
        for n in range(2):
            v = [br[part, pl.ds(4 * n + i, 64, stride=8), :] for i in range(4)]
            u = regroup(v)
            for c in range(2):
                turned = jnp.concatenate([u[2 * c], u[2 * c + 1]], axis=0).T
                for i in range(4):
                    r_v[pl.ds(8 * c + 4 * n + i, 32, stride=16), :] = turned[i * 32 : i * 32 + 32]
        lanes = pl.ds(part * 128, 128)
        return acc[...] + dot3(split(r_v[pl.ds(0, 512), :]), (tbp_hl[0, :, lanes], tbp_hl[1, :, lanes]), LAST)

    for copy in loads[1:6]:
        copy.wait()
    span_stage(0, 0)
    send_fwd(1, 1, 2)
    for i in range(4):
        send_vel(i, 3)
    for copy in loads[6:] + own_vel:
        copy.wait()
    prepare_basis()
    span_stage(1, 0)
    prepare_divisor()
    gradient_stage(0)
    along_stage(0)
    span_stage(0, 1)
    gradient_stage(1)
    along_stage(1)
    span_stage(1, 1)
    prepare_theta()
    span_back_stage(0)
    span_back_stage(1)
    gradient_stage(2)
    along_stage(2)
    gradient_stage(3)
    along_stage(3)
    span_back_stage(2)
    span_back_stage(3)
    acc[...] = collect(0)
    acc[...] = collect(1)
    acc[...] = collect(2)
    c_hl[0], c_hl[1] = split(collect(3) * inv_div[...])
    results = []
    for half in range(2):
        points = pl.ds(half * 256, 256)
        ov[:, points] = dot3((c_hl[0], c_hl[1]), (fb_hl[0, points, :], fb_hl[1, points, :]), LAST)
        results.append(pltpu.make_async_copy(ov.at[:, points], out.at[:, points], out_sem.at[half]))
        results[-1].start()

    for c in range(2):
        for f in range(2):
            wait_all(fs.at[f, c, pl.ds(0, 63)], f_send.at[f, c])
    for part in range(4):
        wait_all(vel_v.at[:, :, pl.ds(0, 32), pl.ds(0, 2)], vel_send.at[part])
        for h in range(3):
            wait_all(xs.at[part, h, pl.ds(0, 384)], x_send.at[part, h])
        wait_all(xbs.at[part, pl.ds(0, 384)], xb_send.at[part])
        wait_all(br.at[part, pl.ds(0, 504)], b_send.at[part])
    for result in results:
        result.wait()


def shards(theta_hat, velocity, wall_derivative, to_basis, from_basis, eigenvalues):
    tables = span_tables() + along_tables()
    tables = [jnp.asarray(t) for t in tables]
    vm = pltpu.VMEM
    table = vm((2, 512, 512), BF16)
    square = vm((512, 512), F32)
    blocked = vm((4, 512, 128), F32)
    dma = pltpu.SemaphoreType.DMA
    result = pl.pallas_call(
        kernel,
        out_shape=jax.ShapeDtypeStruct((512, 512), F32),
        in_specs=[pl.BlockSpec(memory_space=pl.ANY)] * 12,
        out_specs=pl.BlockSpec(memory_space=pl.ANY),
        scratch_shapes=[
            vm((4, 528, 128), F32), blocked, square, square, square, vm((1, 512), F32), vm((3, 4, 65, 8, 128), F32),
            table, table, table, table, table, table,
            table, table, table, table, square,
            vm((2, 2, 64, 16, 128), F32),
            vm((2, 2, 1056, 128), F32),
            vm((2, 512, 256), BF16),
            vm((4, 3, 512, 128), F32),
            vm((4, 3, 512, 128), F32),
            vm((3, 2, 128, 512), BF16),
            vm((2, 3, 128, 512), F32),
            vm((2, 128, 512), BF16),
            vm((4, 512, 128), F32),
            vm((4, 512, 128), F32),
            vm((4, 2, 256, 128), F32),
            vm((4, 520, 128), F32),
            table,
            vm((528, 128), F32),
            vm((512, 512), BF16),
            table,
            square,
            square,
            dma((18,)), dma((4,)), dma((4,)), dma((2, 2)), dma((2, 2)), dma((4, 3)), dma((4, 3)),
            dma((4,)), dma((4,)), dma((4,)), dma((4,)), dma((4,)),
        ],
        compiler_params=pltpu.CompilerParams(
            collective_id=0, has_side_effects=True, vmem_limit_bytes=VMEM_LIMIT
        ),
        cost_estimate=pl.CostEstimate(flops=8 * 10**9, bytes_accessed=16 * 2**20, transcendentals=0),
    )(
        theta_hat.reshape(512, 512), velocity, wall_derivative, to_basis, from_basis,
        eigenvalues.reshape(1, 512), *tables,
    )
    return result.reshape(32, 2, 8, 512)


def solution(mesh):
    return jax.shard_map(
        shards,
        mesh=mesh,
        in_specs=(P("row", None, "col", None), P(None, "row", "col", None), P(), P(), P(), P()),
        out_specs=P("row", None, "col", None),
        check_vma=False,
    )
```
